128 devices in a mesh: dp: 8 (over z, core), sec: 2 (over x_hi), vocab: 8 (over x_lo, y).
Axes of the slice: x: 4 (x_hi: 2, x_lo: 2; x = x_hi * 2 + x_lo), y: 4, z: 4, core: 2. Of those that a mesh axis runs over, the one named last changes fastest.
Arguments:
- teacher_hidden: bfloat16 [2, 256, 4608], P(None, 'dp'), may hold values from -410 to 410
- student_hidden: bfloat16 [2, 256, 3584], P(None, 'dp'), may hold values from -410 to 410
- teacher_gain: float32 [4608], replicated, may hold values from 0.5 to 1.5
- student_gain: float32 [3584], replicated, may hold values from 0.5 to 1.5
- teacher_head: bfloat16 [4608, 131072], P(None, ('dp', 'sec', 'vocab')), may hold values from -2 to 2
- student_head: bfloat16 [3584, 131072], P(None, ('dp', 'sec', 'vocab')), may hold values from -2 to 2
- labels: int32 [2, 256], replicated, may hold values from 0 to 131071
Outputs:
- row_loss: float32 [2, 256], P(None, 'dp')
- grad_hidden: bfloat16 [2, 256, 3584], P(None, 'dp')
- grad_head: bfloat16 [3584, 131072], P(None, ('dp', 'sec', 'vocab'))
The draws below stay inside these ranges and needn't reach their ends.
All inputs are finite; a program needn't handle non-finite values.
Results may differ from the reference program's by a relative error of at most 0.0015.
The reference program's roundings to bfloat16 on the way (of `teacher_normed`, `student_normed` and `logit_grad`) count: a program that leaves them out, or rounds other values in their place, can miss the bound.
Values may be sent and summed in bfloat16 or wider, within the bound.
No kernel may reach another device: no remote copies, remote signals or barrier semaphores. Data moves between devices by JAX's collectives and lax.ppermute only.
A program may use at most 128 MiB of HBM per device.

```python
import math
import jax
import jax.numpy as jnp
import numpy as np
from jax import lax

D_T = 4608
D_S = 3584
ROWS = 256
NMB = 2
V = 131072


def spread_field(base_key, batches, row_total, feature_total):
    normal_key = jax.random.fold_in(base_key, 1)
    row_key = jax.random.fold_in(base_key, 4)
    column_key = jax.random.fold_in(base_key, 5)
    shape = (batches, row_total, feature_total)
    normal_part = jnp.clip(jax.random.normal(normal_key, shape, jnp.float32), -4.0, 4.0)
    row_scale = jnp.exp(jax.random.uniform(row_key, (batches, row_total, 1), jnp.float32, 0.0, math.log(10.0)))
    column_scale = jnp.exp(jax.random.uniform(column_key, (1, 1, feature_total), jnp.float32, 0.0, math.log(10.0)))
    mixed = normal_part
    return (mixed * row_scale * column_scale).astype(jnp.bfloat16)


def offset_head(base_key, feature_total, column_total, offset_limit):
    noise_key = jax.random.fold_in(base_key, 1)
    offset_key = jax.random.fold_in(base_key, 3)
    shape = (feature_total, column_total)
    normal_part = jnp.clip(jax.random.normal(noise_key, shape, jnp.float32), -4.0, 4.0)
    noise = normal_part
    offset = jnp.clip(0.1 * jax.random.normal(offset_key, (feature_total, 1), jnp.float32), -offset_limit, offset_limit)
    scale = 1.5 / math.sqrt(feature_total)
    return (noise * scale + offset).astype(jnp.bfloat16)


def draw_teacher_hidden(key, part):
    key = jax.random.fold_in(key, 11)
    return spread_field(key, NMB, ROWS, D_T)


def draw_student_hidden(key, part):
    key = jax.random.fold_in(key, 23)
    return spread_field(key, NMB, ROWS, D_S)


def draw_teacher_head(key, part):
    key = jax.random.fold_in(key, 31)
    return offset_head(key, D_T, V, 0.25)


def draw_student_head(key, part):
    key = jax.random.fold_in(key, 37)
    return offset_head(key, D_S, V, 0.3125)


def plant(array, key, least, largest):
    index_at = [jax.random.randint(jax.random.fold_in(key, axis), (), 0, length) for axis, length in enumerate(array.shape)]
    longest = array.shape.index(max(array.shape))
    beside = index_at[:longest] + [(index_at[longest] + 1) % array.shape[longest]] + index_at[longest + 1:]
    return array.at[tuple(index_at)].set(least).at[tuple(beside)].set(largest)


def wide_ids(stream_key, extent, amount, slope):
    weights = [min(1 << octave, amount + 1 - (1 << octave)) * (1 << 20) // math.isqrt((1 << octave) ** slope) + 1 for octave in range((amount + 1).bit_length()) if 1 << octave <= amount]
    width = 1 + sum(weights) // (1 << 30)
    table = np.cumsum(np.array([max(1, weight // width) for weight in weights]))
    lot = jax.random.randint(jax.random.fold_in(stream_key, 1), extent, 0, int(table[len(weights) - 1]))
    start = jnp.left_shift(1, jnp.searchsorted(jnp.asarray(table, jnp.int32), lot, side="right").astype(jnp.int32))
    grade = start - 1 + jax.random.randint(jax.random.fold_in(stream_key, 4), extent, 0, 1 << 30) % jnp.minimum(start, amount + 1 - start)
    return jax.random.permutation(jax.random.fold_in(stream_key, 2), amount)[grade].astype(jnp.int32)


def setup_inputs(seed: int = 0) -> dict:
    streams_of = jax.random.split(jax.random.key(seed), 8)
    teacher_hidden = draw_teacher_hidden(jax.random.fold_in(streams_of[7], 71), 0)
    student_hidden = draw_student_hidden(jax.random.fold_in(streams_of[7], 71), 0)
    teacher_gain = jnp.clip(1.0 + 0.1 * jax.random.normal(streams_of[2], (D_T,), jnp.float32), 0.5, 1.5)
    student_gain = jnp.clip(1.0 + 0.1 * jax.random.normal(streams_of[3], (D_S,), jnp.float32), 0.5, 1.5)
    teacher_head = draw_teacher_head(jax.random.fold_in(streams_of[7], 71), 0)
    student_head = draw_student_head(jax.random.fold_in(streams_of[7], 71), 0)
    labels = plant(wide_ids(streams_of[6], (NMB, ROWS), V, 2), jax.random.fold_in(streams_of[6], 3), 0, V - 1).astype(jnp.int32)
    return {"teacher_hidden": teacher_hidden, "student_hidden": student_hidden, "teacher_gain": teacher_gain, "student_gain": student_gain, "teacher_head": teacher_head, "student_head": student_head, "labels": labels}


SOFT_CAP = 30.0
KL_WEIGHT = 0.5
NORM_EPS = 1e-06

def normalize(hidden, gain):
    values = hidden.astype(jnp.float32)
    factor = lax.rsqrt(lax.optimization_barrier(jnp.mean(values * values, axis=-1, keepdims=True)) + NORM_EPS)
    return ((values * factor * gain).astype(jnp.bfloat16), factor)

def capped_logits(normed, head_cols):
    return SOFT_CAP * jnp.tanh(jnp.dot(normed, head_cols, preferred_element_type=jnp.float32) / SOFT_CAP)

def norm_backward(hidden, factor, gain, upstream):
    values = hidden.astype(jnp.float32)
    scaled = upstream * gain
    inner_sum = lax.optimization_barrier(jnp.mean(values * scaled, axis=-1, keepdims=True))
    return factor * scaled - values * (factor * factor * factor) * inner_sum

def reference(teacher_hidden, student_hidden, teacher_gain, student_gain, teacher_head, student_head, labels):
    columns = jnp.arange(V, dtype=jnp.int32)[None, :]
    losses = []
    hidden_grads = []
    normed_parts = []
    grad_parts = []
    for member in range(NMB):
        teacher_normed, _ = normalize(teacher_hidden[member], teacher_gain)
        student_normed, student_factor = normalize(student_hidden[member], student_gain)
        teacher_cap = capped_logits(teacher_normed, teacher_head)
        student_cap = capped_logits(student_normed, student_head)
        teacher_exp = jnp.exp(teacher_cap)
        student_exp = jnp.exp(student_cap)
        matches = labels[member][:, None] == columns
        teacher_total = lax.optimization_barrier(jnp.sum(teacher_exp, axis=1))
        student_total = lax.optimization_barrier(jnp.sum(student_exp, axis=1))
        cross_total = lax.optimization_barrier(jnp.sum(teacher_exp * (teacher_cap - student_cap), axis=1))
        picked_total = lax.optimization_barrier(jnp.sum(jnp.where(matches, student_cap, jnp.float32(0.0)), axis=1))
        divergence = cross_total / teacher_total - jnp.log(teacher_total) + jnp.log(student_total)
        label_term = jnp.log(student_total) - picked_total
        losses.append(KL_WEIGHT * divergence + (1.0 - KL_WEIGHT) * label_term)
        ratio = student_cap / SOFT_CAP
        logit_grad = (student_exp / student_total[:, None] - KL_WEIGHT * teacher_exp / teacher_total[:, None] - (1.0 - KL_WEIGHT) * matches.astype(jnp.float32)) * (1.0 - ratio * ratio)
        logit_grad = logit_grad.astype(jnp.bfloat16)
        upstream = lax.dot_general(logit_grad, student_head, (((1,), (1,)), ((), ())), preferred_element_type=jnp.float32)
        hidden_grads.append(norm_backward(student_hidden[member], student_factor, student_gain, upstream).astype(jnp.bfloat16))
        normed_parts.append(student_normed)
        grad_parts.append(logit_grad)
    normed_all = jnp.concatenate(normed_parts, axis=0)
    grad_all = jnp.concatenate(grad_parts, axis=0)
    grad_head = lax.dot_general(normed_all, grad_all, (((0,), (0,)), ((), ())), preferred_element_type=jnp.float32)
    return (jnp.stack(losses), jnp.stack(hidden_grads), grad_head.astype(jnp.bfloat16))
```

```python
import jax
import jax.numpy as jnp
from jax import lax
from jax.sharding import PartitionSpec as P

SOFT_CAP = 30.0
KL_WEIGHT = 0.5
NORM_EPS = 1e-06
AXES = ("dp", "sec", "vocab")
PLANE = ("sec", "vocab")
CHIPS = [[(2 * z + core) * 16 + place for z in range(4) for place in range(16)] for core in range(2)]
SIBLING = [(i, i ^ 1) for i in range(8)]


def row_factor(values):
    return lax.rsqrt(jnp.mean(values * values, axis=-1, keepdims=True) + NORM_EPS)


def capped_logits(normed, head_cols):
    return SOFT_CAP * jnp.tanh(
        jnp.dot(normed, head_cols, preferred_element_type=jnp.float32) / SOFT_CAP
    )


def back_rows(logit_rows, head_cols):
    return lax.dot_general(
        logit_rows, head_cols, (((1,), (1,)), ((), ())), preferred_element_type=jnp.float32
    )


def sum_everywhere(part):
    chip = part + lax.ppermute(part, "dp", SIBLING)
    copies = jnp.broadcast_to(chip.reshape(1, 8, 128), (64, 8, 128))
    got = lax.all_to_all(copies, AXES, 0, 0, tiled=True, axis_index_groups=CHIPS)
    return jnp.sum(got, axis=0).reshape(part.shape)


def body(
    teacher_hidden, student_hidden, teacher_gain, student_gain, teacher_head, student_head, labels
):
    batches, local_rows, d_t = teacher_hidden.shape
    d_s = student_hidden.shape[2]
    col_count = student_head.shape[1]
    device_place = lax.axis_index(AXES)
    columns = device_place * col_count + lax.broadcasted_iota(jnp.int32, (1, col_count), 1)
    dp = lax.axis_index("dp")
    core = dp % 2
    teacher_values = teacher_hidden.astype(jnp.float32)
    student_values = student_hidden.astype(jnp.float32)
    teacher_own = (teacher_values * row_factor(teacher_values) * teacher_gain).astype(jnp.bfloat16)
    student_factor = row_factor(student_values)
    student_own = (student_values * student_factor * student_gain).astype(jnp.bfloat16)
    both_own = jnp.concatenate([teacher_own, student_own], axis=2)
    losses, hidden_grads, normed_parts, grad_parts = [], [], [], []
    for member in range(batches):
        rows = lax.all_gather(both_own[member], "dp", axis=0, tiled=True)
        student_normed = rows[:, d_t:]
        teacher_cap = capped_logits(rows[:, :d_t], teacher_head)
        student_cap = capped_logits(student_normed, student_head)
        teacher_exp = jnp.exp(teacher_cap)
        student_exp = jnp.exp(student_cap)
        matches = labels[member][:, None] == columns
        part = jnp.stack(
            [
                jnp.sum(teacher_exp, axis=1),
                jnp.sum(student_exp, axis=1),
                jnp.sum(teacher_exp * (teacher_cap - student_cap), axis=1),
                jnp.sum(jnp.where(matches, student_cap, jnp.float32(0.0)), axis=1),
            ]
        )
        totals = sum_everywhere(part)
        teacher_total, student_total = totals[0], totals[1]
        ratio = student_cap / SOFT_CAP
        logit_grad = (
            student_exp / student_total[:, None]
            - KL_WEIGHT * teacher_exp / teacher_total[:, None]
            - (1.0 - KL_WEIGHT) * matches.astype(jnp.float32)
        ) * (1.0 - ratio * ratio)
        logit_grad = logit_grad.astype(jnp.bfloat16)
        normed_parts.append(student_normed)
        grad_parts.append(logit_grad)
        by_core = logit_grad.reshape(4, 2, local_rows, col_count)
        theirs = lax.dynamic_index_in_dim(by_core, 1 - core, 1, keepdims=False)
        mine = lax.dynamic_index_in_dim(by_core, core, 1, keepdims=False)
        theirs_up = back_rows(theirs.reshape(4 * local_rows, col_count), student_head)
        chip_up = back_rows(mine.reshape(4 * local_rows, col_count), student_head)
        chip_up = chip_up + lax.ppermute(theirs_up, "dp", SIBLING)
        pieces = chip_up.reshape(4, 4, 8, 4, d_s // 4).transpose(0, 3, 1, 2, 4)
        pieces = pieces.reshape(64, 8, d_s // 4)
        got = lax.all_to_all(pieces, AXES, 0, 0, tiled=True, axis_index_groups=CHIPS)
        piece = jnp.sum(got, axis=0)
        spread = jnp.broadcast_to(piece[None], (16, 8, d_s // 4))
        spread = lax.all_to_all(spread, PLANE, 0, 0, tiled=True)
        upstream = spread.reshape(4, 4, 8, d_s // 4).transpose(1, 2, 0, 3).reshape(local_rows, d_s)
        factor = student_factor[member]
        values = student_values[member]
        scaled = upstream * student_gain
        inner_sum = jnp.mean(values * scaled, axis=-1, keepdims=True)
        hidden_grads.append(
            (factor * scaled - values * (factor * factor * factor) * inner_sum).astype(jnp.bfloat16)
        )
        own = lax.dynamic_slice_in_dim(totals, dp * local_rows, local_rows, 1)
        divergence = own[2] / own[0] - jnp.log(own[0]) + jnp.log(own[1])
        losses.append(KL_WEIGHT * divergence + (1.0 - KL_WEIGHT) * (jnp.log(own[1]) - own[3]))
    head_grad = lax.dot_general(
        jnp.concatenate(normed_parts, axis=0),
        jnp.concatenate(grad_parts, axis=0),
        (((0,), (0,)), ((), ())),
        preferred_element_type=jnp.float32,
    )
    return (jnp.stack(losses), jnp.stack(hidden_grads), head_grad.astype(jnp.bfloat16))


def solution(mesh):
    in_specs = (
        P(None, "dp", None),
        P(None, "dp", None),
        P(),
        P(),
        P(None, AXES),
        P(None, AXES),
        P(),
    )
    out_specs = (P(None, "dp"), P(None, "dp", None), P(None, AXES))
    return jax.shard_map(body, mesh=mesh, in_specs=in_specs, out_specs=out_specs, check_vma=False)
```

```python
import functools

import jax
import jax.numpy as jnp
from jax import lax
from jax.experimental import pallas as pl
from jax.experimental.pallas import tpu as pltpu
from jax.sharding import PartitionSpec as P

SOFT_CAP = 30.0
KL_WEIGHT = 0.5
NORM_EPS = 1e-06
AXES = ("dp", "sec", "vocab")
D_T, D_S, COLS = 4608, 3584, 1024
D_ALL = D_T + D_S
OWN = 64
ROWS = 8 * OWN
HALF = D_ALL // 2
QUARTER = HALF // 4
LANES = 896
FINISH_COPIES = 4
HEAD_STEPS = 7
MIB = 1024 * 1024


def linear(z, core, x, y):
    return (2 * z + core) * 16 + 4 * x + y


def pairs(move):
    return [
        (linear(z, c, x, y), linear(*move(z, c, x, y)))
        for z in range(4)
        for c in range(2)
        for x in range(4)
        for y in range(4)
    ]


SIBLING = pairs(lambda z, c, x, y: (z, 1 - c, x, y))
ALONG_Z = [pairs(lambda z, c, x, y, d=d: ((z + d) % 4, c, x, y)) for d in range(4)]
ALONG_LINE = [
    pairs(lambda z, c, x, y, e=e: (z, c, x, (y + e) % 4) if c else (z, c, (x + e) % 4, y))
    for e in range(4)
]
CHIPS = [
    [linear(z, c, x, y) for z in range(4) for x in range(4) for y in range(4)] for c in range(2)
]


LINES = [[linear(z, 0, x, y) for x in range(4)] for z in range(4) for y in range(4)] + [
    [linear(z, 1, x, y) for y in range(4)] for z in range(4) for x in range(4)
]
WALLS = [[linear(z, 0, x, y) for z in range(4) for y in range(4)] for x in range(4)] + [
    [linear(z, 1, x, y) for z in range(4) for x in range(4)] for y in range(4)
]
PLANES = [[linear(z, 0, x, y) for x in range(4) for y in range(4)] for z in range(4)] + [
    [linear(z, 1, x, y) for y in range(4) for x in range(4)] for z in range(4)
]


def swap(value):
    return lax.ppermute(value, AXES, SIBLING)


def norm_kernel(place, teacher, student, teacher_gain, student_gain, own, quarter):
    def normed(ref, gain):
        values = ref[...].astype(jnp.float32)
        factor = lax.rsqrt(jnp.mean(values * values, axis=-1, keepdims=True) + NORM_EPS)
        return (values * factor * gain[...][None, :]).astype(jnp.bfloat16)

    own[:, :D_T] = normed(teacher, teacher_gain)
    own[:, D_T:] = normed(student, student_gain)
    start = pl.multiple_of(place[2] * QUARTER, QUARTER)
    quarter[0] = own[:, pl.ds(start, QUARTER)]
    quarter[1] = own[:, pl.ds(HALF + start, QUARTER)]


def collect(place, half, pieces, rows, sems):
    z, core, line, line_s = place[0], place[1], place[2], place[3]
    mine, theirs = pieces[:5], pieces[5:]
    groups = []
    for k, (other, at, (own, near, *lines)) in enumerate(
        ((core, line, mine), (1 - core, line_s, theirs))
    ):

        def block(far):
            return pl.ds(pl.multiple_of((other * 4 + (z + 4 - far) % 4) * OWN, OWN), OWN)

        todo = [(own.at[:, pl.ds(half * HALF, HALF)], rows.at[block(0)])]
        for far in range(1, 4):
            for e in range(4):
                lanes = pl.ds(pl.multiple_of(((at + 4 - e) % 4) * QUARTER, QUARTER), QUARTER)
                source = near.at[half, far - 1] if e == 0 else lines[e - 1].at[far - 1]
                todo.append((source, rows.at[block(far), lanes]))
        groups.append(
            [pltpu.make_async_copy(a, b, sems.at[13 * k + i]) for i, (a, b) in enumerate(todo)]
        )
    return groups


def begin(copies):
    for copy in copies:
        copy.start()


def finish(copies):
    for copy in copies:
        copy.wait()


TILE = 256


def head_tiles(parts, buffers, sems):
    def copies(n):
        out, at = [], 0
        for k, (head, start, count) in enumerate(parts):
            source = head.at[pl.ds(start, count), pl.ds(TILE * n, TILE)]
            target = buffers.at[n % 2, pl.ds(at, count), :]
            out.append(pltpu.make_async_copy(source, target, sems.at[n % 2, k]))
            at += count
        return out

    def start(n):
        if n < COLS // TILE:
            for copy in copies(n):
                copy.start()

    def wait(n):
        for copy in copies(n):
            copy.wait()

    return start, wait


def core_rows(core):
    return pl.ds(pl.multiple_of(core * (ROWS // 2), ROWS // 2), ROWS // 2)


def first_kernel(place, *refs):
    *pieces, teacher_head, teacher_part, rows, heads, sems, head_sems = refs
    start, wait = head_tiles([(teacher_head, 0, HALF)], heads, head_sems)
    groups = collect(place, 0, pieces, rows, sems)
    begin(groups[0])
    start(0)
    begin(groups[1])
    start(1)
    for n in range(COLS // TILE):
        tile = slice(TILE * n, TILE * n + TILE)
        if n == 0:
            finish(groups[0])
            wait(0)
            for k in range(2):
                if k:
                    finish(groups[1])
                at = core_rows(place[1] if k == 0 else 1 - place[1])
                teacher_part[at, tile] = jnp.dot(
                    rows[at, :], heads[0], preferred_element_type=jnp.float32
                )
        else:
            wait(n)
            teacher_part[:, tile] = jnp.dot(
                rows[...], heads[n % 2], preferred_element_type=jnp.float32
            )
        start(n + 2)


def second_kernel(place, *refs):
    *pieces, teacher_part, teacher_head, student_head, labels = refs[:14]
    teacher_out, student_out, sums = refs[14:17]
    rows, heads, teacher_exp, student_cap, acc, sems, head_sems, out_sems = refs[17:]
    rest = D_T - HALF
    start, wait = head_tiles(
        [(teacher_head, HALF, rest), (student_head, 0, D_S)], heads, head_sems
    )
    groups = collect(place, 1, pieces, rows, sems)
    begin(groups[0])
    start(0)
    begin(groups[1])
    start(1)
    acc[...] = jnp.zeros_like(acc)

    def fold(value):
        return sum(value[:, 128 * i : 128 * i + 128] for i in range(TILE // 128))

    def dots(n, at):
        tile = slice(TILE * n, TILE * n + TILE)
        teacher_exp[n, at, :] = teacher_part[at, tile] + jnp.dot(
            rows[at, :rest], heads[n % 2, :rest, :], preferred_element_type=jnp.float32
        )
        student_cap[n, at, :] = jnp.dot(
            rows[at, rest:], heads[n % 2, rest:, :], preferred_element_type=jnp.float32
        )

    out_copies = []

    def caps(n):
        columns = place[4] + TILE * n + lax.broadcasted_iota(jnp.int32, (1, TILE), 1)
        chunk = 32
        for i in range(ROWS // chunk):
            at = slice(chunk * i, chunk * i + chunk)
            t_cap = SOFT_CAP * jnp.tanh(teacher_exp[n, at, :] * (1.0 / SOFT_CAP))
            s_cap = SOFT_CAP * jnp.tanh(student_cap[n, at, :] * (1.0 / SOFT_CAP))
            t_exp = jnp.exp(t_cap)
            teacher_exp[n, at, :] = t_exp
            student_cap[n, at, :] = s_cap
            picked = jnp.where(labels[at, :] == columns, s_cap, jnp.float32(0.0))
            acc[0, at, :] += fold(t_exp)
            acc[1, at, :] += fold(jnp.exp(s_cap))
            acc[2, at, :] += fold(t_exp * (t_cap - s_cap))
            acc[3, at, :] += fold(picked)
        for k, (source, out) in enumerate(((teacher_exp, teacher_out), (student_cap, student_out))):
            copy = pltpu.make_async_copy(
                source.at[n], out.at[:, pl.ds(TILE * n, TILE)], out_sems.at[2 * n + k]
            )
            copy.start()
            out_copies.append(copy)

    for n in range(COLS // TILE):
        if n == 0:
            finish(groups[0])
            wait(0)
            dots(0, core_rows(place[1]))
            finish(groups[1])
            dots(0, core_rows(1 - place[1]))
        else:
            wait(n)
            dots(n, slice(0, ROWS))
            caps(n - 1)
        start(n + 2)
    caps(COLS // TILE - 1)
    for kind in range(4):
        for i in range(4):
            block = acc[kind, 128 * i : 128 * i + 128, :]
            at = 4 * kind + i
            sums[at : at + 1, :] = jnp.sum(block.T, axis=0, keepdims=True)
    finish(out_copies)


def grad_kernel(
    place, teacher_in, student_in, totals, labels, logit_grad, teacher_exp, student_cap, sems
):
    copies = []
    for i in range(4):
        at = pl.ds(128 * i, 128)
        copies.append(
            [
                pltpu.make_async_copy(teacher_in.at[at, :], teacher_exp.at[at, :], sems.at[i, 0]),
                pltpu.make_async_copy(student_in.at[at, :], student_cap.at[at, :], sems.at[i, 1]),
            ]
        )
        for copy in copies[-1]:
            copy.start()
    columns = place[4] + lax.broadcasted_iota(jnp.int32, (1, COLS), 1)
    for i in range(4):

        def column(kind):
            at = 4 * kind + i
            return jnp.broadcast_to(totals[at : at + 1, :], (128, 128)).T

        teacher_scale = KL_WEIGHT / column(0)
        student_scale = 1.0 / column(1)
        block = slice(128 * i, 128 * i + 128)
        label = labels[block, :]
        for copy in copies[i]:
            copy.wait()
        for j in range(COLS // 128):
            lanes = slice(128 * j, 128 * j + 128)
            s_cap = student_cap[block, lanes]
            ratio = s_cap * (1.0 / SOFT_CAP)
            matches = (label == columns[:, lanes]).astype(jnp.float32)
            grad = (
                jnp.exp(s_cap) * student_scale
                - teacher_exp[block, lanes] * teacher_scale
                - (1.0 - KL_WEIGHT) * matches
            ) * (1.0 - ratio * ratio)
            logit_grad[2 * i, :, lanes] = grad[:OWN].astype(jnp.bfloat16)
            logit_grad[2 * i + 1, :, lanes] = grad[OWN:].astype(jnp.bfloat16)


def back_dot(logit_grad, core, head, part, n):
    rows = logit_grad[pl.ds(4 * core, 4)].reshape(4 * OWN, COLS)
    start = part * (D_S // 2) + n * LANES
    return lax.dot_general(
        rows,
        head[start : start + LANES, :],
        (((1,), (1,)), ((), ())),
        preferred_element_type=jnp.float32,
    )


def head_grad_kernel(place, *refs):
    *pieces, logit_grad, out, rows, buffers, sems, out_sems = refs
    groups = collect(place, 1, pieces, rows, sems)
    for group in groups:
        begin(group)
    for group in groups:
        finish(group)
    step = D_S // HEAD_STEPS

    def copy_out(n):
        return pltpu.make_async_copy(
            buffers.at[n % 2], out.at[pl.ds(step * n, step), :], out_sems.at[n % 2]
        )

    for n in range(HEAD_STEPS):
        lanes = slice(D_T - HALF + step * n, D_T - HALF + step * n + step)
        value = lax.dot_general(
            rows[:, lanes],
            logit_grad[...].reshape(ROWS, COLS),
            (((0,), (0,)), ((), ())),
            preferred_element_type=jnp.float32,
        )
        if n >= 2:
            copy_out(n - 2).wait()
        buffers[n % 2] = value.astype(jnp.bfloat16)
        copy_out(n).start()
    for n in range(HEAD_STEPS - 2, HEAD_STEPS):
        copy_out(n).wait()


def theirs_kernel(part, place, logit_grad, head, out):
    for n in range(D_S // 2 // LANES):
        out[:, n * LANES : n * LANES + LANES] = back_dot(logit_grad, 1 - place[1], head, part, n)


def mine_kernel(part, place, logit_grad, head, received, *rest):
    out = rest[-1]
    for n in range(D_S // 2 // LANES):
        lanes = slice(n * LANES, n * LANES + LANES)
        value = back_dot(logit_grad, place[1], head, part, n) + received[:, lanes]
        start = part * (D_S // 2) + n * LANES
        for i in range(64):
            to = (i // 4 % 4) * 16 + (i // 16) * 4 + i % 4
            out[to, :, start : start + LANES] = value[4 * i : 4 * i + 4, :]


def line_sum_kernel(got, out, parts, total, sems, out_sems):
    def copy_in(i, source):
        at = pl.ds(16 * source + 4 * i, 4)
        return pltpu.make_async_copy(got.at[at], parts.at[at], sems.at[i, source])

    def copy_out(i):
        at = pl.ds(4 * i, 4)
        return pltpu.make_async_copy(total.at[at], out.at[at], out_sems.at[i])

    for i in range(4):
        for source in range(4):
            copy_in(i, source).start()
    for i in range(4):
        for source in range(4):
            copy_in(i, source).wait()
        for k in range(4 * i, 4 * i + 4):
            total[k] = (parts[k] + parts[16 + k]) + (parts[32 + k] + parts[48 + k])
        copy_out(i).start()
    for i in range(4):
        copy_out(i).wait()


def finish_kernel(got, hidden, gain, out, parts, sems):
    chunk = 16 // FINISH_COPIES
    copies = [
        pltpu.make_async_copy(got.at[pl.ds(chunk * i, chunk)], parts.at[i], sems.at[i])
        for i in range(FINISH_COPIES)
    ]
    for copy in copies:
        copy.start()
    total = None
    for i in range(FINISH_COPIES):
        copies[i].wait()
        for k in range(chunk):
            part = parts[i, k]
            total = part if total is None else total + part
    values = hidden[...].astype(jnp.float32)
    factor = lax.rsqrt(jnp.mean(values * values, axis=-1, keepdims=True) + NORM_EPS)
    scaled = total * gain[...][None, :]
    inner_sum = jnp.mean(values * scaled, axis=-1, keepdims=True)
    grad = factor * scaled - values * (factor * factor * factor) * inner_sum
    out[...] = jnp.broadcast_to(grad.astype(jnp.bfloat16)[None], out.shape)


def limit(mib):
    return pltpu.CompilerParams(vmem_limit_bytes=mib * MIB)


def in_hbm(value):
    return pltpu.with_memory_space_constraint(value, pltpu.HBM)


def sum_everywhere(part):
    chip = part + swap(part)
    copies = jnp.broadcast_to(chip[None], (64, 16, 128))
    got = lax.all_to_all(copies, AXES, 0, 0, tiled=True, axis_index_groups=CHIPS)
    return jnp.sum(got, axis=0)


def body(
    teacher_hidden, student_hidden, teacher_gain, student_gain, teacher_head, student_head, labels
):
    dp, sec, vocab = (lax.axis_index(a) for a in AXES)
    z, core = dp // 2, dp % 2
    x, y = sec * 2 + vocab // 4, vocab % 4
    line = jnp.where(core == 0, x, y)
    line_s = other = jnp.where(core == 0, y, x)
    device_place = lax.axis_index(AXES)
    place = jnp.stack([z, core, line, line_s, device_place * COLS, 1 - core]).astype(jnp.int32)
    labels_here = labels.reshape(2, 4, 2, 32).transpose(2, 1, 0, 3).reshape(ROWS, 1)

    smem = pl.BlockSpec(memory_space=pltpu.SMEM)
    vmem = pl.BlockSpec(memory_space=pltpu.VMEM)
    any_space = pl.BlockSpec(memory_space=pltpu.HBM)
    own, quarter = pl.pallas_call(
        norm_kernel,
        out_shape=[
            jax.ShapeDtypeStruct((OWN, D_ALL), jnp.bfloat16),
            jax.ShapeDtypeStruct((2, OWN, QUARTER), jnp.bfloat16),
        ],
        in_specs=[smem] + [vmem] * 4,
        out_specs=[vmem] * 2,
        compiler_params=limit(56),
    )(
        place,
        teacher_hidden.reshape(OWN, D_T),
        student_hidden.reshape(OWN, D_S),
        teacher_gain,
        student_gain,
    )

    own_s = swap(own)

    near = jnp.stack([lax.ppermute(quarter, AXES, ALONG_Z[d]) for d in (1, 2, 3)], axis=1)
    near, own_s = lax.optimization_barrier((near, own_s))
    lines_1, lines_2 = (
        [lax.ppermute(near[half], AXES, ALONG_LINE[e]) for e in (1, 2, 3)] for half in range(2)
    )
    near_s, lines_1[0] = lax.optimization_barrier((near, lines_1[0]))
    near_s = swap(near_s)
    pieces_1 = [own, near, *lines_1, own_s, near_s, *(swap(v) for v in lines_1)]
    teacher_part = pl.pallas_call(
        first_kernel,
        out_shape=jax.ShapeDtypeStruct((ROWS, COLS), jnp.float32),
        in_specs=[smem] + [any_space] * 11,
        out_specs=vmem,
        scratch_shapes=[
            pltpu.VMEM((ROWS, HALF), jnp.bfloat16),
            pltpu.VMEM((2, HALF, TILE), jnp.bfloat16),
            pltpu.SemaphoreType.DMA((26,)),
            pltpu.SemaphoreType.DMA((2, 1)),
        ],
        compiler_params=limit(24),
        cost_estimate=pl.CostEstimate(
            flops=2 * ROWS * HALF * COLS, bytes_accessed=14 * MIB, transcendentals=0
        ),
    )(place, *map(in_hbm, pieces_1), in_hbm(teacher_head))
    *lines_2, teacher_part = lax.optimization_barrier((*lines_2, teacher_part))
    pieces_2 = [own, near, *lines_2, own_s, near_s, *(swap(v) for v in lines_2)]
    teacher_exp, student_cap, sums = pl.pallas_call(
        second_kernel,
        out_shape=[
            pltpu.HBM((ROWS, COLS), jnp.float32),
            pltpu.HBM((ROWS, COLS), jnp.float32),
            jax.ShapeDtypeStruct((16, 128), jnp.float32),
        ],
        in_specs=[smem] + [any_space] * 10 + [vmem] + [any_space] * 2 + [vmem],
        out_specs=[any_space] * 2 + [vmem],
        scratch_shapes=[
            pltpu.VMEM((ROWS, HALF), jnp.bfloat16),
            pltpu.VMEM((2, HALF, TILE), jnp.bfloat16),
            pltpu.VMEM((COLS // TILE, ROWS, TILE), jnp.float32),
            pltpu.VMEM((COLS // TILE, ROWS, TILE), jnp.float32),
            pltpu.VMEM((4, ROWS, 128), jnp.float32),
            pltpu.SemaphoreType.DMA((26,)),
            pltpu.SemaphoreType.DMA((2, 2)),
            pltpu.SemaphoreType.DMA((8,)),
        ],
        compiler_params=limit(28),
        cost_estimate=pl.CostEstimate(
            flops=2 * ROWS * HALF * COLS, bytes_accessed=24 * MIB, transcendentals=4 * ROWS * COLS
        ),
    )(
        place,
        *map(in_hbm, pieces_2),
        teacher_part,
        in_hbm(teacher_head),
        in_hbm(student_head),
        labels_here,
    )

    totals = sum_everywhere(sums)

    logit_grad = pl.pallas_call(
        grad_kernel,
        out_shape=jax.ShapeDtypeStruct((8, OWN, COLS), jnp.bfloat16),
        in_specs=[smem] + [any_space] * 2 + [vmem] * 2,
        out_specs=vmem,
        scratch_shapes=[
            pltpu.VMEM((ROWS, COLS), jnp.float32),
            pltpu.VMEM((ROWS, COLS), jnp.float32),
            pltpu.SemaphoreType.DMA((4, 2)),
        ],
        compiler_params=limit(10),
        cost_estimate=pl.CostEstimate(
            flops=8 * ROWS * COLS, bytes_accessed=5 * MIB, transcendentals=ROWS * COLS
        ),
    )(
        place, in_hbm(teacher_exp), in_hbm(student_cap), totals, labels_here
    )

    back_cost = pl.CostEstimate(
        flops=4 * OWN * COLS * D_S, bytes_accessed=6 * MIB, transcendentals=0
    )
    theirs = [
        swap(
            pl.pallas_call(
                functools.partial(theirs_kernel, part),
                out_shape=jax.ShapeDtypeStruct((4 * OWN, D_S // 2), jnp.float32),
                in_specs=[smem, vmem, vmem],
                out_specs=vmem,
                compiler_params=limit(6),
                cost_estimate=back_cost,
            )(place, logit_grad, student_head)
        )
        for part in range(2)
    ]
    pieces = ()
    for part in range(2):
        pieces = pl.pallas_call(
            functools.partial(mine_kernel, part),
            out_shape=[jax.ShapeDtypeStruct((64, 4, D_S), jnp.float32)],
            in_specs=[smem, vmem, vmem, vmem] + [vmem] * part,
            out_specs=[vmem],
            input_output_aliases={4: 0} if part else {},
            compiler_params=limit(8),
            cost_estimate=back_cost,
        )(place, logit_grad, student_head, theirs[part], *pieces)
    got = lax.all_to_all(pieces[0], AXES, 0, 0, tiled=True, axis_index_groups=LINES)
    head_grad = pl.pallas_call(
        head_grad_kernel,
        out_shape=pltpu.HBM((D_S, COLS), jnp.bfloat16),
        in_specs=[smem] + [any_space] * 10 + [vmem],
        out_specs=any_space,
        scratch_shapes=[
            pltpu.VMEM((ROWS, HALF), jnp.bfloat16),
            pltpu.VMEM((2, D_S // HEAD_STEPS, COLS), jnp.bfloat16),
            pltpu.SemaphoreType.DMA((26,)),
            pltpu.SemaphoreType.DMA((2,)),
        ],
        compiler_params=limit(20),
        cost_estimate=pl.CostEstimate(
            flops=2 * ROWS * D_S * COLS, bytes_accessed=13 * MIB, transcendentals=0
        ),
    )(place, *map(in_hbm, pieces_2), logit_grad)
    got, head_grad = lax.optimization_barrier((got, head_grad))
    got = pl.pallas_call(
        line_sum_kernel,
        out_shape=pltpu.HBM((16, 4, D_S), jnp.float32),
        in_specs=[any_space],
        out_specs=any_space,
        scratch_shapes=[
            pltpu.VMEM((64, 4, D_S), jnp.float32),
            pltpu.VMEM((16, 4, D_S), jnp.float32),
            pltpu.SemaphoreType.DMA((4, 4)),
            pltpu.SemaphoreType.DMA((4,)),
        ],
        compiler_params=limit(12),
    )(in_hbm(got))
    got = lax.all_to_all(got, AXES, 0, 0, tiled=True, axis_index_groups=WALLS)
    hidden = student_hidden.reshape(16, 4, D_S)
    hidden = lax.dynamic_index_in_dim(hidden, 4 * line + other, 0, keepdims=False)
    hidden_grad = pl.pallas_call(
        finish_kernel,
        out_shape=jax.ShapeDtypeStruct((16, 4, D_S), jnp.bfloat16),
        in_specs=[any_space, vmem, vmem],
        out_specs=vmem,
        scratch_shapes=[
            pltpu.VMEM((FINISH_COPIES, 16 // FINISH_COPIES, 4, D_S), jnp.float32),
            pltpu.SemaphoreType.DMA((FINISH_COPIES,)),
        ],
        compiler_params=limit(8),
    )(in_hbm(got), hidden, student_gain)
    hidden_grad = lax.all_to_all(hidden_grad, AXES, 0, 0, tiled=True, axis_index_groups=PLANES)

    mine = lax.dynamic_slice_in_dim(totals.reshape(4, ROWS), (4 * core + z) * OWN, OWN, 1)
    divergence = mine[2] / mine[0] - jnp.log(mine[0]) + jnp.log(mine[1])
    loss = KL_WEIGHT * divergence + (1.0 - KL_WEIGHT) * (jnp.log(mine[1]) - mine[3])
    return (loss.reshape(2, 32), hidden_grad.reshape(2, 32, D_S), head_grad)


def solution(mesh):
    in_specs = (
        P(None, "dp", None),
        P(None, "dp", None),
        P(),
        P(),
        P(None, AXES),
        P(None, AXES),
        P(),
    )
    out_specs = (P(None, "dp"), P(None, "dp", None), P(None, AXES))
    return jax.shard_map(body, mesh=mesh, in_specs=in_specs, out_specs=out_specs, check_vma=False)
```

```python
import functools

import jax
import jax.numpy as jnp
from jax import lax
from jax.experimental import pallas as pl
from jax.experimental.pallas import tpu as pltpu
from jax.sharding import PartitionSpec as P

SOFT_CAP = 30.0
KL_WEIGHT = 0.5
NORM_EPS = 1e-06
AXES = ("dp", "sec", "vocab")
D_T, D_S, COLS = 4608, 3584, 1024
D_ALL = D_T + D_S
OWN = 64
ROWS = 8 * OWN
QUARTER = D_ALL // 4
NEAR, FAR = (0, 1, 3), (2,)
FARS = NEAR + FAR
LANES = 896
HEAD_STEPS = 7
MIB = 1024 * 1024


def linear(z, core, x, y):
    return (2 * z + core) * 16 + 4 * x + y


def pairs(move):
    return [
        (linear(z, c, x, y), linear(*move(z, c, x, y)))
        for z in range(4)
        for c in range(2)
        for x in range(4)
        for y in range(4)
    ]


SIBLING = pairs(lambda z, c, x, y: (z, 1 - c, x, y))
ALONG_Z = [pairs(lambda z, c, x, y, d=d: ((z + d) % 4, c, x, y)) for d in range(4)]
ALONG_LINE = [
    pairs(lambda z, c, x, y, e=e: (z, c, x, (y + e) % 4) if c else (z, c, (x + e) % 4, y))
    for e in range(4)
]
CHIPS = [
    [linear(z, c, x, y) for z in range(4) for x in range(4) for y in range(4)] for c in range(2)
]


WALLS = [[linear(z, 0, x, y) for z in range(4) for y in range(4)] for x in range(4)] + [
    [linear(z, 1, x, y) for z in range(4) for x in range(4)] for y in range(4)
]
PLANES = [[linear(z, 0, x, y) for x in range(4) for y in range(4)] for z in range(4)] + [
    [linear(z, 1, x, y) for y in range(4) for x in range(4)] for z in range(4)
]


def swap(value):
    return lax.ppermute(value, AXES, SIBLING)


def norm_kernel(*refs):
    inputs, (own, quarter), buffers, sems = refs[:4], refs[4:6], refs[6:10], refs[10]
    copies = [pltpu.make_async_copy(a, b, sems.at[i]) for i, (a, b) in enumerate(zip(inputs, buffers))]
    begin(copies)
    teacher, student, teacher_gain, student_gain = buffers

    def normed(ref, gain):
        values = ref[...].astype(jnp.float32)
        factor = lax.rsqrt(jnp.mean(values * values, axis=-1, keepdims=True) + NORM_EPS)
        return (values * factor * gain[...][None, :]).astype(jnp.bfloat16)

    finish([copies[1], copies[3]])
    own[:, D_T:] = normed(student, student_gain)
    finish([copies[0], copies[2]])
    own[:, :D_T] = normed(teacher, teacher_gain)
    dp, sec, vocab = (lax.axis_index(a) for a in AXES)
    line = jnp.where(dp % 2 == 0, sec * 2 + vocab // 4, vocab % 4)
    quarter[...] = own[:, pl.ds(pl.multiple_of(line * QUARTER, QUARTER), QUARTER)]


def row_start(place, k, far):
    other = place[1] if k == 0 else 1 - place[1]
    return pl.multiple_of((other * 4 + (place[0] + 4 - far) % 4) * OWN, OWN)


def collect(place, pieces, rows, start_of, sems):
    groups, used = ([], []), 0
    for k, far, sources in pieces:
        block = pl.ds(start_of(k, far), OWN)
        for e, source in enumerate(sources):
            target = rows.at[block]
            if len(sources) > 1:
                lanes = pl.multiple_of(((place[2 + k] + 4 - e) % 4) * QUARTER, QUARTER)
                target = rows.at[block, pl.ds(lanes, QUARTER)]
            groups[k].append(pltpu.make_async_copy(source, target, sems.at[used]))
            used += 1
    return groups


def pieces_of(fars, refs):
    out, per_core = [], len(refs) // 2
    for k in range(2):
        own, lines = refs[k * per_core], refs[(k + 1) * per_core - 4 : (k + 1) * per_core]
        others = [far for far in fars if far]
        for far in fars:
            if far == 0:
                out.append((k, far, [own]))
            else:
                out.append((k, far, [line.at[others.index(far)] for line in lines]))
    return out


def begin(copies):
    for copy in copies:
        copy.start()


def finish(copies):
    for copy in copies:
        copy.wait()


CHUNK = 1024
BUFFERS = 3


def head_chunks(parts, buffers, sems):
    def copy(n):
        head, start, count = parts[n]
        target = buffers.at[n % BUFFERS, pl.ds(0, count), :]
        return pltpu.make_async_copy(head.at[pl.ds(start, count), :], target, sems.at[n % BUFFERS])

    def start(n):
        if n < len(parts):
            copy(n).start()

    return start, lambda n: copy(n).wait()


def all_pieces(refs):
    return pieces_of(NEAR, refs[:10]) + pieces_of(FAR, refs[10:18])


def forward_kernel(place, *refs):
    received, refs = refs[:18], refs[18:]
    teacher_head, student_head, labels = refs[:3]
    teacher_out, student_out, sums = refs[3:6]
    rows, heads, teacher_cap, teacher_exp, student_cap, acc, sems, head_sems, out_sems = refs[6:]
    side = len(FARS) * OWN
    parts = [(teacher_head, at, min(CHUNK, D_T - at)) for at in range(0, D_T, CHUNK)]
    teacher_parts = len(parts)
    parts += [(student_head, at, min(CHUNK, D_S - at)) for at in range(0, D_S, CHUNK)]
    start, wait = head_chunks(parts, heads, head_sems)
    groups = collect(
        place, all_pieces(received), rows, lambda k, far: k * side + FARS.index(far) * OWN, sems
    )
    begin(groups[0])
    start(0)
    begin(groups[1])
    start(1)
    start(2)

    def fold(value):
        return sum(value[:, 128 * i : 128 * i + 128] for i in range(COLS // 128))

    blocks = [(k, far) for k in range(2) for far in FARS]

    def out_copy(source, out, k, b):
        there = pl.ds(row_start(place, *blocks[b]), OWN)
        return pltpu.make_async_copy(source.at[pl.ds(OWN * b, OWN), :], out.at[there, :], out_sems.at[k, b])

    step = 16
    columns = place[4] + lax.broadcasted_iota(jnp.int32, (1, COLS), 1)

    def steps_of(b):
        first = row_start(place, *blocks[b])
        for i in range(OWN // step):
            at = OWN * b + step * i
            yield slice(at, at + step), pl.ds(pl.multiple_of(first + step * i, step), step)

    def teacher_block(b):
        for at, there in steps_of(b):
            t_cap = SOFT_CAP * jnp.tanh(teacher_cap[at, :] * (1.0 / SOFT_CAP))
            t_exp = jnp.exp(t_cap)
            teacher_cap[at, :] = t_cap
            teacher_exp[at, :] = t_exp
            acc[0, there, :] = fold(t_exp)
        out_copy(teacher_exp, teacher_out, 0, b).start()

    def student_block(b):
        for at, there in steps_of(b):
            s_cap = SOFT_CAP * jnp.tanh(student_cap[at, :] * (1.0 / SOFT_CAP))
            student_cap[at, :] = s_cap
            picked = jnp.where(labels[there, :] == columns, s_cap, jnp.float32(0.0))
            acc[1, there, :] = fold(jnp.exp(s_cap))
            acc[2, there, :] = fold(teacher_exp[at, :] * (teacher_cap[at, :] - s_cap))
            acc[3, there, :] = fold(picked)
        out_copy(student_cap, student_out, 1, b).start()

    lane, done = 0, 0
    for n, (_, _, count) in enumerate(parts):
        lanes = slice(lane, lane + count)
        lane += count
        total = teacher_cap if n < teacher_parts else student_cap
        if n == 0:
            for k in range(2):
                finish(groups[k])
                if k == 0:
                    wait(0)
                at = slice(k * side, k * side + side)
                total[at, :] = jnp.dot(
                    rows[at, lanes], heads[0, :count, :], preferred_element_type=jnp.float32
                )
        else:
            wait(n)
            value = jnp.dot(
                rows[:, lanes], heads[n % BUFFERS, :count, :], preferred_element_type=jnp.float32
            )
            total[...] = value if n == teacher_parts else total[...] + value
        if n >= teacher_parts:
            until = len(blocks) * (n + 1 - teacher_parts) // (len(parts) - teacher_parts)
            for b in range(done, until):
                teacher_block(b)
            done = until
        start(n + BUFFERS)
    for b in range(len(blocks)):
        student_block(b)
    for kind in range(4):
        for i in range(4):
            block = acc[kind, 128 * i : 128 * i + 128, :]
            at = 4 * kind + i
            sums[at : at + 1, :] = jnp.sum(block.T, axis=0, keepdims=True)
    for b in range(len(blocks)):
        out_copy(teacher_exp, teacher_out, 0, b).wait()
        out_copy(student_cap, student_out, 1, b).wait()


def grad_kernel(
    place, teacher_in, student_in, totals, labels, head, logit_grad, head_here,
    teacher_exp, student_cap, sems, head_sem,
):
    copies = []
    for i in range(4):
        at = pl.ds(128 * i, 128)
        copies.append(
            [
                pltpu.make_async_copy(teacher_in.at[at, :], teacher_exp.at[at, :], sems.at[i, 0]),
                pltpu.make_async_copy(student_in.at[at, :], student_cap.at[at, :], sems.at[i, 1]),
            ]
        )
        begin(copies[-1])
    head_copy = pltpu.make_async_copy(head, head_here, head_sem)
    head_copy.start()
    columns = place[4] + lax.broadcasted_iota(jnp.int32, (1, COLS), 1)
    for i in range(4):

        def column(kind):
            at = 4 * kind + i
            return jnp.broadcast_to(totals[at : at + 1, :], (128, 128)).T

        teacher_scale = KL_WEIGHT / column(0)
        student_scale = 1.0 / column(1)
        block = slice(128 * i, 128 * i + 128)
        label = labels[block, :]
        finish(copies[i])
        for j in range(COLS // 128):
            lanes = slice(128 * j, 128 * j + 128)
            s_cap = student_cap[block, lanes]
            ratio = s_cap * (1.0 / SOFT_CAP)
            matches = (label == columns[:, lanes]).astype(jnp.float32)
            grad = (
                jnp.exp(s_cap) * student_scale
                - teacher_exp[block, lanes] * teacher_scale
                - (1.0 - KL_WEIGHT) * matches
            ) * (1.0 - ratio * ratio)
            logit_grad[2 * i, :, lanes] = grad[:OWN].astype(jnp.bfloat16)
            logit_grad[2 * i + 1, :, lanes] = grad[OWN:].astype(jnp.bfloat16)
    head_copy.wait()


def back_dot(logit_grad, core, head, part, n):
    rows = logit_grad[pl.ds(4 * core, 4)].reshape(4 * OWN, COLS)
    start = part * (D_S // 2) + n * LANES
    return lax.dot_general(
        rows,
        head[start : start + LANES, :],
        (((1,), (1,)), ((), ())),
        preferred_element_type=jnp.float32,
    )


def head_grad_kernel(place, *refs):
    received = refs[:18]
    logit_grad, out, rows, buffers, sems, out_sems = refs[18:]
    groups = collect(place, all_pieces(received), rows, functools.partial(row_start, place), sems)
    for group in groups:
        begin(group)
    for group in groups:
        finish(group)
    step = D_S // HEAD_STEPS

    def copy_out(n):
        return pltpu.make_async_copy(
            buffers.at[n % 2], out.at[pl.ds(step * n, step), :], out_sems.at[n % 2]
        )

    for n in range(HEAD_STEPS):
        lanes = slice(D_T + step * n, D_T + step * n + step)
        value = lax.dot_general(
            rows[:, lanes],
            logit_grad[...].reshape(ROWS, COLS),
            (((0,), (0,)), ((), ())),
            preferred_element_type=jnp.float32,
        )
        if n >= 2:
            copy_out(n - 2).wait()
        buffers[n % 2] = value.astype(jnp.bfloat16)
        copy_out(n).start()
    for n in range(HEAD_STEPS - 2, HEAD_STEPS):
        copy_out(n).wait()


def theirs_kernel(part, place, logit_grad, head, out):
    for n in range(D_S // 2 // LANES):
        out[:, n * LANES : n * LANES + LANES] = back_dot(logit_grad, 1 - place[1], head, part, n)


def mine_kernel(part, place, logit_grad, head, received, *rest):
    *outs, value = rest
    for n in range(D_S // 2 // LANES):
        lanes = slice(n * LANES, n * LANES + LANES)
        value[...] = back_dot(logit_grad, place[1], head, part, n) + received[:, lanes]
        for e, out in enumerate(outs):
            for z in range(4):
                at = pl.multiple_of(z * OWN + ((place[2] + e) % 4) * 16, 16)
                block = value[pl.ds(at, 16), :]
                for other in range(4):
                    out[4 * z + other, :, lanes] = block[4 * other : 4 * other + 4]


def line_sum_kernel(*refs):
    slabs, (out, total, sems) = refs[:8], refs[8:]

    def copy_out(i):
        at = pl.ds(4 * i, 4)
        return pltpu.make_async_copy(total.at[at], out.at[at], sems.at[i])

    for i in range(4):
        for part in range(2):
            a, b, c, d = slabs[4 * part : 4 * part + 4]
            lanes = slice(part * (D_S // 2), (part + 1) * (D_S // 2))
            for at in range(4 * i, 4 * i + 4):
                total[at, :, lanes] = (a[at] + b[at]) + (c[at] + d[at])
        copy_out(i).start()
    for i in range(4):
        copy_out(i).wait()


def finish_kernel(got, hidden, gain, out):
    total = got[0]
    for k in range(1, 16):
        total = total + got[k]
    values = hidden[...].astype(jnp.float32)
    factor = lax.rsqrt(jnp.mean(values * values, axis=-1, keepdims=True) + NORM_EPS)
    scaled = total * gain[...][None, :]
    inner_sum = jnp.mean(values * scaled, axis=-1, keepdims=True)
    grad = factor * scaled - values * (factor * factor * factor) * inner_sum
    out[...] = jnp.broadcast_to(grad.astype(jnp.bfloat16)[None], out.shape)


def limit(mib):
    return pltpu.CompilerParams(vmem_limit_bytes=mib * MIB)


def in_hbm(value):
    return pltpu.with_memory_space_constraint(value, pltpu.HBM)


def sum_everywhere(part):
    chip = part + swap(part)
    copies = jnp.broadcast_to(chip[None], (64, 16, 128))
    got = lax.all_to_all(copies, AXES, 0, 0, tiled=True, axis_index_groups=CHIPS)
    return jnp.sum(got, axis=0)


def body(
    teacher_hidden, student_hidden, teacher_gain, student_gain, teacher_head, student_head, labels
):
    dp, sec, vocab = (lax.axis_index(a) for a in AXES)
    z, core = dp // 2, dp % 2
    x, y = sec * 2 + vocab // 4, vocab % 4
    line = jnp.where(core == 0, x, y)
    line_s = other = jnp.where(core == 0, y, x)
    device_place = lax.axis_index(AXES)
    place = jnp.stack([z, core, line, line_s, device_place * COLS, 1 - core]).astype(jnp.int32)
    labels_here = labels.reshape(2, 4, 2, 32).transpose(2, 1, 0, 3).reshape(ROWS, 1)

    smem = pl.BlockSpec(memory_space=pltpu.SMEM)
    vmem = pl.BlockSpec(memory_space=pltpu.VMEM)
    any_space = pl.BlockSpec(memory_space=pltpu.HBM)
    own, quarter = pl.pallas_call(
        norm_kernel,
        out_shape=[
            jax.ShapeDtypeStruct((OWN, D_ALL), jnp.bfloat16),
            jax.ShapeDtypeStruct((OWN, QUARTER), jnp.bfloat16),
        ],
        in_specs=[any_space] * 4,
        out_specs=[vmem] * 2,
        scratch_shapes=[
            pltpu.VMEM((OWN, D_T), jnp.bfloat16),
            pltpu.VMEM((OWN, D_S), jnp.bfloat16),
            pltpu.VMEM((D_T,), jnp.float32),
            pltpu.VMEM((D_S,), jnp.float32),
            pltpu.SemaphoreType.DMA((4,)),
        ],
        compiler_params=limit(10),
    )(
        in_hbm(teacher_hidden.reshape(OWN, D_T)),
        in_hbm(student_hidden.reshape(OWN, D_S)),
        in_hbm(teacher_gain),
        in_hbm(student_gain),
    )

    own_s = swap(own)

    next_1, next_3, opposite = (lax.ppermute(quarter, AXES, ALONG_Z[d]) for d in (1, 3, 2))
    near, own_s = lax.optimization_barrier((jnp.stack([next_1, next_3]), own_s))

    def along_line(value):
        return [value] + [lax.ppermute(value, AXES, ALONG_LINE[e]) for e in (1, 2, 3)]

    near_lines = along_line(near)
    far_lines = along_line(opposite[None])
    pieces = [own, *near_lines, own_s, *map(swap, near_lines), *far_lines, *map(swap, far_lines)]
    teacher_exp, student_cap, sums = pl.pallas_call(
        forward_kernel,
        out_shape=[
            pltpu.HBM((ROWS, COLS), jnp.float32),
            pltpu.HBM((ROWS, COLS), jnp.float32),
            jax.ShapeDtypeStruct((16, 128), jnp.float32),
        ],
        in_specs=[smem] + [any_space] * 20 + [vmem],
        out_specs=[any_space] * 2 + [vmem],
        scratch_shapes=[
            pltpu.VMEM((ROWS, D_ALL), jnp.bfloat16),
            pltpu.VMEM((BUFFERS, CHUNK, COLS), jnp.bfloat16),
            pltpu.VMEM((ROWS, COLS), jnp.float32),
            pltpu.VMEM((ROWS, COLS), jnp.float32),
            pltpu.VMEM((ROWS, COLS), jnp.float32),
            pltpu.VMEM((4, ROWS, 128), jnp.float32),
            pltpu.SemaphoreType.DMA((26,)),
            pltpu.SemaphoreType.DMA((BUFFERS,)),
            pltpu.SemaphoreType.DMA((2, 8)),
        ],
        compiler_params=limit(32),
        cost_estimate=pl.CostEstimate(
            flops=2 * ROWS * D_ALL * COLS, bytes_accessed=30 * MIB, transcendentals=4 * ROWS * COLS
        ),
    )(
        place,
        *map(in_hbm, pieces),
        in_hbm(teacher_head),
        in_hbm(student_head),
        labels_here,
    )

    totals = sum_everywhere(sums)

    logit_grad, head_here = pl.pallas_call(
        grad_kernel,
        out_shape=[
            jax.ShapeDtypeStruct((8, OWN, COLS), jnp.bfloat16),
            jax.ShapeDtypeStruct((D_S, COLS), jnp.bfloat16),
        ],
        in_specs=[smem] + [any_space] * 2 + [vmem] * 2 + [any_space],
        out_specs=[vmem] * 2,
        scratch_shapes=[
            pltpu.VMEM((ROWS, COLS), jnp.float32),
            pltpu.VMEM((ROWS, COLS), jnp.float32),
            pltpu.SemaphoreType.DMA((4, 2)),
            pltpu.SemaphoreType.DMA,
        ],
        compiler_params=limit(10),
        cost_estimate=pl.CostEstimate(
            flops=8 * ROWS * COLS, bytes_accessed=5 * MIB, transcendentals=ROWS * COLS
        ),
    )(
        place, in_hbm(teacher_exp), in_hbm(student_cap), totals, labels_here,
        in_hbm(student_head),
    )

    back_cost = pl.CostEstimate(
        flops=4 * OWN * COLS * D_S, bytes_accessed=6 * MIB, transcendentals=0
    )
    theirs = [
        swap(
            pl.pallas_call(
                functools.partial(theirs_kernel, part),
                out_shape=jax.ShapeDtypeStruct((4 * OWN, D_S // 2), jnp.float32),
                in_specs=[smem, vmem, vmem],
                out_specs=vmem,
                compiler_params=limit(6),
                cost_estimate=back_cost,
            )(place, logit_grad, head_here)
        )
        for part in range(2)
    ]
    slabs = []
    for part in range(2):
        mine = pl.pallas_call(
            functools.partial(mine_kernel, part),
            out_shape=[jax.ShapeDtypeStruct((16, 4, D_S // 2), jnp.float32)] * 4,
            in_specs=[smem, vmem, vmem, vmem],
            out_specs=[vmem] * 4,
            scratch_shapes=[pltpu.VMEM((4 * OWN, LANES), jnp.float32)],
            compiler_params=limit(8),
            cost_estimate=back_cost,
        )(place, logit_grad, head_here, theirs[part])
        slabs += [mine[0]] + [lax.ppermute(mine[e], AXES, ALONG_LINE[e]) for e in (1, 2, 3)]
    head_grad = pl.pallas_call(
        head_grad_kernel,
        out_shape=pltpu.HBM((D_S, COLS), jnp.bfloat16),
        in_specs=[smem] + [any_space] * 18 + [vmem],
        out_specs=any_space,
        scratch_shapes=[
            pltpu.VMEM((ROWS, D_ALL), jnp.bfloat16),
            pltpu.VMEM((2, D_S // HEAD_STEPS, COLS), jnp.bfloat16),
            pltpu.SemaphoreType.DMA((26,)),
            pltpu.SemaphoreType.DMA((2,)),
        ],
        compiler_params=limit(20),
        cost_estimate=pl.CostEstimate(
            flops=2 * ROWS * D_S * COLS, bytes_accessed=13 * MIB, transcendentals=0
        ),
    )(place, *map(in_hbm, pieces), logit_grad)
    *slabs, head_grad = lax.optimization_barrier((*slabs, head_grad))
    got = pl.pallas_call(
        line_sum_kernel,
        out_shape=pltpu.HBM((16, 4, D_S), jnp.float32),
        in_specs=[vmem] * 8,
        out_specs=any_space,
        scratch_shapes=[
            pltpu.VMEM((16, 4, D_S), jnp.float32),
            pltpu.SemaphoreType.DMA((4,)),
        ],
        compiler_params=limit(6),
    )(*slabs)
    got = lax.all_to_all(got, AXES, 0, 0, tiled=True, axis_index_groups=WALLS)
    hidden = student_hidden.reshape(16, 4, D_S)
    hidden = lax.dynamic_index_in_dim(hidden, 4 * line + other, 0, keepdims=False)
    hidden_grad = pl.pallas_call(
        finish_kernel,
        out_shape=jax.ShapeDtypeStruct((16, 4, D_S), jnp.bfloat16),
        in_specs=[vmem] * 3,
        out_specs=vmem,
        compiler_params=limit(4),
    )(got, hidden, student_gain)
    hidden_grad = lax.all_to_all(hidden_grad, AXES, 0, 0, tiled=True, axis_index_groups=PLANES)

    mine = lax.dynamic_slice_in_dim(totals.reshape(4, ROWS), (4 * core + z) * OWN, OWN, 1)
    divergence = mine[2] / mine[0] - jnp.log(mine[0]) + jnp.log(mine[1])
    loss = KL_WEIGHT * divergence + (1.0 - KL_WEIGHT) * (jnp.log(mine[1]) - mine[3])
    return (loss.reshape(2, 32), hidden_grad.reshape(2, 32, D_S), head_grad)


def solution(mesh):
    in_specs = (
        P(None, "dp", None),
        P(None, "dp", None),
        P(),
        P(),
        P(None, AXES),
        P(None, AXES),
        P(),
    )
    out_specs = (P(None, "dp"), P(None, "dp", None), P(None, AXES))
    return jax.shard_map(body, mesh=mesh, in_specs=in_specs, out_specs=out_specs, check_vma=False)
```

```python
import functools

import jax
import jax.numpy as jnp
from jax import lax
from jax.experimental import pallas as pl
from jax.experimental.pallas import tpu as pltpu
from jax.sharding import PartitionSpec as P

SOFT_CAP = 30.0
KL_WEIGHT = 0.5
NORM_EPS = 1e-06
AXES = ("dp", "sec", "vocab")
D_T, D_S, COLS = 4608, 3584, 1024
D_ALL = D_T + D_S
OWN = 64
ROWS = 8 * OWN
QUARTER = D_ALL // 4
NEAR, FAR = (0, 1, 3), (2,)
FARS = NEAR + FAR
LANES = 896
HEAD_STEPS = 7
MIB = 1024 * 1024


def linear(z, core, x, y):
    return (2 * z + core) * 16 + 4 * x + y


def pairs(move):
    return [
        (linear(z, c, x, y), linear(*move(z, c, x, y)))
        for z in range(4)
        for c in range(2)
        for x in range(4)
        for y in range(4)
    ]


SIBLING = pairs(lambda z, c, x, y: (z, 1 - c, x, y))
ALONG_Z = [pairs(lambda z, c, x, y, d=d: ((z + d) % 4, c, x, y)) for d in range(4)]
ALONG_LINE = [
    pairs(lambda z, c, x, y, e=e: (z, c, x, (y + e) % 4) if c else (z, c, (x + e) % 4, y))
    for e in range(4)
]
CHIPS = [
    [linear(z, c, x, y) for z in range(4) for x in range(4) for y in range(4)] for c in range(2)
]


WALLS = [[linear(z, 0, x, y) for z in range(4) for y in range(4)] for x in range(4)] + [
    [linear(z, 1, x, y) for z in range(4) for x in range(4)] for y in range(4)
]
PLANES = [[linear(z, 0, x, y) for x in range(4) for y in range(4)] for z in range(4)] + [
    [linear(z, 1, x, y) for y in range(4) for x in range(4)] for z in range(4)
]


def swap(value):
    return lax.ppermute(value, AXES, SIBLING)


def norm_kernel(*refs):
    inputs, (own, quarter), buffers, sems = refs[:4], refs[4:6], refs[6:10], refs[10]
    copies = [pltpu.make_async_copy(a, b, sems.at[i]) for i, (a, b) in enumerate(zip(inputs, buffers))]
    begin(copies)
    teacher, student, teacher_gain, student_gain = buffers

    def normed(ref, gain):
        values = ref[...].astype(jnp.float32)
        factor = lax.rsqrt(jnp.mean(values * values, axis=-1, keepdims=True) + NORM_EPS)
        return (values * factor * gain[...][None, :]).astype(jnp.bfloat16)

    finish([copies[1], copies[3]])
    own[:, D_T:] = normed(student, student_gain)
    finish([copies[0], copies[2]])
    own[:, :D_T] = normed(teacher, teacher_gain)
    dp, sec, vocab = (lax.axis_index(a) for a in AXES)
    line = jnp.where(dp % 2 == 0, sec * 2 + vocab // 4, vocab % 4)
    quarter[...] = own[:, pl.ds(pl.multiple_of(line * QUARTER, QUARTER), QUARTER)]


def row_start(place, k, far):
    other = place[1] if k == 0 else 1 - place[1]
    return pl.multiple_of((other * 4 + (place[0] + 4 - far) % 4) * OWN, OWN)


def collect(place, pieces, rows, start_of, sems):
    groups, used = ([], []), 0
    for k, far, sources in pieces:
        block = pl.ds(start_of(k, far), OWN)
        for e, source in enumerate(sources):
            target = rows.at[block]
            if len(sources) > 1:
                lanes = pl.multiple_of(((place[2 + k] + 4 - e) % 4) * QUARTER, QUARTER)
                target = rows.at[block, pl.ds(lanes, QUARTER)]
            groups[k].append(pltpu.make_async_copy(source, target, sems.at[used]))
            used += 1
    return groups


def pieces_of(fars, refs):
    out, per_core = [], len(refs) // 2
    for k in range(2):
        own, lines = refs[k * per_core], refs[(k + 1) * per_core - 4 : (k + 1) * per_core]
        others = [far for far in fars if far]
        for far in fars:
            if far == 0:
                out.append((k, far, [own]))
            else:
                out.append((k, far, [line.at[others.index(far)] for line in lines]))
    return out


def begin(copies):
    for copy in copies:
        copy.start()


def finish(copies):
    for copy in copies:
        copy.wait()


CHUNK = 1024
BUFFERS = 3


def head_chunks(parts, buffers, sems):
    def copy(n):
        head, start, count = parts[n]
        target = buffers.at[n % BUFFERS, pl.ds(0, count), :]
        return pltpu.make_async_copy(head.at[pl.ds(start, count), :], target, sems.at[n % BUFFERS])

    def start(n):
        if n < len(parts):
            copy(n).start()

    return start, lambda n: copy(n).wait()


def all_pieces(refs):
    return pieces_of(NEAR, refs[:10]) + pieces_of(FAR, refs[10:18])


def forward_kernel(place, *refs):
    received, refs = refs[:18], refs[18:]
    teacher_head, student_head, labels = refs[:3]
    teacher_out, student_out, sums = refs[3:6]
    rows, heads, teacher_cap, teacher_exp, student_cap, acc, sems, head_sems, out_sems = refs[6:]
    side = len(FARS) * OWN
    parts = [(teacher_head, at, min(CHUNK, D_T - at)) for at in range(0, D_T, CHUNK)]
    teacher_parts = len(parts)
    parts += [(student_head, at, min(CHUNK, D_S - at)) for at in range(0, D_S, CHUNK)]
    start, wait = head_chunks(parts, heads, head_sems)
    groups = collect(
        place, all_pieces(received), rows, lambda k, far: k * side + FARS.index(far) * OWN, sems
    )
    begin(groups[0])
    start(0)
    begin(groups[1])
    start(1)
    start(2)

    def fold(value):
        return sum(value[:, 128 * i : 128 * i + 128] for i in range(COLS // 128))

    blocks = [(k, far) for k in range(2) for far in FARS]

    def out_copy(source, out, k, b):
        there = pl.ds(row_start(place, *blocks[b]), OWN)
        return pltpu.make_async_copy(source.at[pl.ds(OWN * b, OWN), :], out.at[there, :], out_sems.at[k, b])

    step = 16
    columns = place[4] + lax.broadcasted_iota(jnp.int32, (1, COLS), 1)

    def steps_of(b):
        first = row_start(place, *blocks[b])
        for i in range(OWN // step):
            at = OWN * b + step * i
            yield slice(at, at + step), pl.ds(pl.multiple_of(first + step * i, step), step)

    def teacher_block(b):
        for at, there in steps_of(b):
            t_cap = SOFT_CAP * jnp.tanh(teacher_cap[at, :] * (1.0 / SOFT_CAP))
            t_exp = jnp.exp(t_cap)
            teacher_cap[at, :] = t_cap
            teacher_exp[at, :] = t_exp
            acc[0, there, :] = fold(t_exp)
        out_copy(teacher_exp, teacher_out, 0, b).start()

    def student_block(b):
        for at, there in steps_of(b):
            s_cap = SOFT_CAP * jnp.tanh(student_cap[at, :] * (1.0 / SOFT_CAP))
            student_cap[at, :] = s_cap
            picked = jnp.where(labels[there, :] == columns, s_cap, jnp.float32(0.0))
            acc[1, there, :] = fold(jnp.exp(s_cap))
            acc[2, there, :] = fold(teacher_exp[at, :] * (teacher_cap[at, :] - s_cap))
            acc[3, there, :] = fold(picked)
        out_copy(student_cap, student_out, 1, b).start()

    lane, done = 0, 0
    for n, (_, _, count) in enumerate(parts):
        lanes = slice(lane, lane + count)
        lane += count
        total = teacher_cap if n < teacher_parts else student_cap
        if n == 0:
            for k in range(2):
                finish(groups[k])
                if k == 0:
                    wait(0)
                at = slice(k * side, k * side + side)
                total[at, :] = jnp.dot(
                    rows[at, lanes], heads[0, :count, :], preferred_element_type=jnp.float32
                )
        else:
            wait(n)
            value = jnp.dot(
                rows[:, lanes], heads[n % BUFFERS, :count, :], preferred_element_type=jnp.float32
            )
            total[...] = value if n == teacher_parts else total[...] + value
        if n >= teacher_parts:
            until = len(blocks) * (n + 1 - teacher_parts) // (len(parts) - teacher_parts)
            for b in range(done, until):
                teacher_block(b)
            done = until
        start(n + BUFFERS)
    for b in range(len(blocks)):
        student_block(b)
    for kind in range(4):
        for i in range(4):
            block = acc[kind, 128 * i : 128 * i + 128, :]
            at = 4 * kind + i
            sums[at : at + 1, :] = jnp.sum(block.T, axis=0, keepdims=True)
    for b in range(len(blocks)):
        out_copy(teacher_exp, teacher_out, 0, b).wait()
        out_copy(student_cap, student_out, 1, b).wait()


def back_dot(logit_grad, head, n):
    return lax.dot_general(
        logit_grad[...].reshape(4 * OWN, COLS),
        head[n * LANES : n * LANES + LANES, :],
        (((1,), (1,)), ((), ())),
        preferred_element_type=jnp.float32,
    )


def grad_kernel(part, place, teacher_in, student_in, totals, labels, head, *refs):
    logit_grad, head_here, out, teacher_exp, student_cap, sems, head_sem = refs[part:]
    other = place[1] if part else 1 - place[1]
    first = pl.multiple_of(other * (ROWS // 2), ROWS // 2)
    copies = []
    for i in range(2):
        at, here = pl.ds(pl.multiple_of(first + 128 * i, 128), 128), pl.ds(128 * i, 128)
        copies.append(
            [
                pltpu.make_async_copy(teacher_in.at[at, :], teacher_exp.at[here, :], sems.at[i, 0]),
                pltpu.make_async_copy(student_in.at[at, :], student_cap.at[here, :], sems.at[i, 1]),
            ]
        )
    head_copy = pltpu.make_async_copy(
        head.at[pl.ds(part * (D_S // 2), D_S // 2), :], head_here, head_sem
    )

    def upstream(rows):
        head_copy.wait()
        for n in range(D_S // 2 // LANES):
            out[:, n * LANES : n * LANES + LANES] = back_dot(rows, head_here, n)

    if part:
        head_copy.start()
        for group in copies:
            begin(group)
        upstream(refs[0])
    else:
        for group in copies:
            begin(group)
        head_copy.start()
    columns = place[4] + lax.broadcasted_iota(jnp.int32, (1, COLS), 1)
    for i in range(2):

        def column(kind):
            row = totals[pl.ds(4 * kind + 2 * other + i, 1), :]
            return jnp.broadcast_to(row, (128, 128)).T

        teacher_scale = KL_WEIGHT / column(0)
        student_scale = 1.0 / column(1)
        block = slice(128 * i, 128 * i + 128)
        label = labels[pl.ds(pl.multiple_of(first + 128 * i, 128), 128), :]
        finish(copies[i])
        for j in range(COLS // 128):
            lanes = slice(128 * j, 128 * j + 128)
            s_cap = student_cap[block, lanes]
            ratio = s_cap * (1.0 / SOFT_CAP)
            matches = (label == columns[:, lanes]).astype(jnp.float32)
            grad = (
                jnp.exp(s_cap) * student_scale
                - teacher_exp[block, lanes] * teacher_scale
                - (1.0 - KL_WEIGHT) * matches
            ) * (1.0 - ratio * ratio)
            logit_grad[2 * i, :, lanes] = grad[:OWN].astype(jnp.bfloat16)
            logit_grad[2 * i + 1, :, lanes] = grad[OWN:].astype(jnp.bfloat16)
    if not part:
        upstream(logit_grad)


def head_grad_kernel(place, *refs):
    received = refs[:18]
    mine, theirs, out, rows, logit_grad, buffers, sems, out_sems = refs[18:]
    side = len(FARS) * OWN
    groups = collect(
        place,
        all_pieces(received),
        rows,
        lambda k, far: k * side + pl.multiple_of((place[0] + 4 - far) % 4 * OWN, OWN),
        sems,
    )
    for group in groups:
        begin(group)
    logit_grad[:side, :] = mine[...].reshape(side, COLS)
    logit_grad[side:, :] = theirs[...].reshape(side, COLS)
    for group in groups:
        finish(group)
    step = D_S // HEAD_STEPS

    def copy_out(n):
        return pltpu.make_async_copy(
            buffers.at[n % 2], out.at[pl.ds(step * n, step), :], out_sems.at[n % 2]
        )

    for n in range(HEAD_STEPS):
        lanes = slice(D_T + step * n, D_T + step * n + step)
        value = lax.dot_general(
            rows[:, lanes],
            logit_grad[...],
            (((0,), (0,)), ((), ())),
            preferred_element_type=jnp.float32,
        )
        if n >= 2:
            copy_out(n - 2).wait()
        buffers[n % 2] = value.astype(jnp.bfloat16)
        copy_out(n).start()
    for n in range(HEAD_STEPS - 2, HEAD_STEPS):
        copy_out(n).wait()


def mine_kernel(place, logit_grad, head, received, *rest):
    *outs, value = rest
    for n in range(D_S // 2 // LANES):
        lanes = slice(n * LANES, n * LANES + LANES)
        value[...] = back_dot(logit_grad, head, n) + received[:, lanes]
        for e, out in enumerate(outs):
            for z in range(4):
                at = pl.multiple_of(z * OWN + ((place[2] + e) % 4) * 16, 16)
                block = value[pl.ds(at, 16), :]
                for other in range(4):
                    out[4 * z + other, :, lanes] = block[4 * other : 4 * other + 4]


def line_sum_kernel(*refs):
    slabs, (out, total, sems) = refs[:8], refs[8:]

    def copy_out(i):
        at = pl.ds(4 * i, 4)
        return pltpu.make_async_copy(total.at[at], out.at[at], sems.at[i])

    for i in range(4):
        for part in range(2):
            a, b, c, d = slabs[4 * part : 4 * part + 4]
            lanes = slice(part * (D_S // 2), (part + 1) * (D_S // 2))
            for at in range(4 * i, 4 * i + 4):
                total[at, :, lanes] = (a[at] + b[at]) + (c[at] + d[at])
        copy_out(i).start()
    for i in range(4):
        copy_out(i).wait()


def finish_kernel(got, hidden, gain, out):
    total = got[0]
    for k in range(1, 16):
        total = total + got[k]
    values = hidden[...].astype(jnp.float32)
    factor = lax.rsqrt(jnp.mean(values * values, axis=-1, keepdims=True) + NORM_EPS)
    scaled = total * gain[...][None, :]
    inner_sum = jnp.mean(values * scaled, axis=-1, keepdims=True)
    grad = factor * scaled - values * (factor * factor * factor) * inner_sum
    out[...] = jnp.broadcast_to(grad.astype(jnp.bfloat16)[None], out.shape)


def limit(mib):
    return pltpu.CompilerParams(vmem_limit_bytes=mib * MIB)


def in_hbm(value):
    return pltpu.with_memory_space_constraint(value, pltpu.HBM)


def sum_everywhere(part):
    chip = part + swap(part)
    copies = jnp.broadcast_to(chip[None], (64, 16, 128))
    got = lax.all_to_all(copies, AXES, 0, 0, tiled=True, axis_index_groups=CHIPS)
    return jnp.sum(got, axis=0)


def body(
    teacher_hidden, student_hidden, teacher_gain, student_gain, teacher_head, student_head, labels
):
    dp, sec, vocab = (lax.axis_index(a) for a in AXES)
    z, core = dp // 2, dp % 2
    x, y = sec * 2 + vocab // 4, vocab % 4
    line = jnp.where(core == 0, x, y)
    line_s = other = jnp.where(core == 0, y, x)
    device_place = lax.axis_index(AXES)
    place = jnp.stack([z, core, line, line_s, device_place * COLS, 1 - core]).astype(jnp.int32)
    labels_here = labels.reshape(2, 4, 2, 32).transpose(2, 1, 0, 3).reshape(ROWS, 1)

    smem = pl.BlockSpec(memory_space=pltpu.SMEM)
    vmem = pl.BlockSpec(memory_space=pltpu.VMEM)
    any_space = pl.BlockSpec(memory_space=pltpu.HBM)
    own, quarter = pl.pallas_call(
        norm_kernel,
        out_shape=[
            jax.ShapeDtypeStruct((OWN, D_ALL), jnp.bfloat16),
            jax.ShapeDtypeStruct((OWN, QUARTER), jnp.bfloat16),
        ],
        in_specs=[any_space] * 4,
        out_specs=[vmem] * 2,
        scratch_shapes=[
            pltpu.VMEM((OWN, D_T), jnp.bfloat16),
            pltpu.VMEM((OWN, D_S), jnp.bfloat16),
            pltpu.VMEM((D_T,), jnp.float32),
            pltpu.VMEM((D_S,), jnp.float32),
            pltpu.SemaphoreType.DMA((4,)),
        ],
        compiler_params=limit(10),
    )(
        in_hbm(teacher_hidden.reshape(OWN, D_T)),
        in_hbm(student_hidden.reshape(OWN, D_S)),
        in_hbm(teacher_gain),
        in_hbm(student_gain),
    )

    own_s = swap(own)

    next_1, next_3, opposite = (lax.ppermute(quarter, AXES, ALONG_Z[d]) for d in (1, 3, 2))
    near, own_s = lax.optimization_barrier((jnp.stack([next_1, next_3]), own_s))

    def along_line(value):
        return [value] + [lax.ppermute(value, AXES, ALONG_LINE[e]) for e in (1, 2, 3)]

    near_lines = along_line(near)
    far_lines = along_line(opposite[None])
    pieces = [own, *near_lines, own_s, *map(swap, near_lines), *far_lines, *map(swap, far_lines)]
    teacher_exp, student_cap, sums = pl.pallas_call(
        forward_kernel,
        out_shape=[
            pltpu.HBM((ROWS, COLS), jnp.float32),
            pltpu.HBM((ROWS, COLS), jnp.float32),
            jax.ShapeDtypeStruct((16, 128), jnp.float32),
        ],
        in_specs=[smem] + [any_space] * 20 + [vmem],
        out_specs=[any_space] * 2 + [vmem],
        scratch_shapes=[
            pltpu.VMEM((ROWS, D_ALL), jnp.bfloat16),
            pltpu.VMEM((BUFFERS, CHUNK, COLS), jnp.bfloat16),
            pltpu.VMEM((ROWS, COLS), jnp.float32),
            pltpu.VMEM((ROWS, COLS), jnp.float32),
            pltpu.VMEM((ROWS, COLS), jnp.float32),
            pltpu.VMEM((4, ROWS, 128), jnp.float32),
            pltpu.SemaphoreType.DMA((26,)),
            pltpu.SemaphoreType.DMA((BUFFERS,)),
            pltpu.SemaphoreType.DMA((2, 8)),
        ],
        compiler_params=limit(32),
        cost_estimate=pl.CostEstimate(
            flops=2 * ROWS * D_ALL * COLS, bytes_accessed=30 * MIB, transcendentals=4 * ROWS * COLS
        ),
    )(
        place,
        *map(in_hbm, pieces),
        in_hbm(teacher_head),
        in_hbm(student_head),
        labels_here,
    )

    totals = sum_everywhere(sums)

    back_cost = pl.CostEstimate(
        flops=4 * OWN * COLS * D_S, bytes_accessed=6 * MIB, transcendentals=ROWS * COLS // 2
    )
    grads, heads_here, theirs = [], [], []
    for part in range(2):
        grad, head_here, out = pl.pallas_call(
            functools.partial(grad_kernel, part),
            out_shape=[
                jax.ShapeDtypeStruct((4, OWN, COLS), jnp.bfloat16),
                jax.ShapeDtypeStruct((D_S // 2, COLS), jnp.bfloat16),
                jax.ShapeDtypeStruct((4 * OWN, D_S // 2), jnp.float32),
            ],
            in_specs=[smem] + [any_space] * 2 + [vmem] * 2 + [any_space] + [vmem] * part,
            out_specs=[vmem] * 3,
            scratch_shapes=[
                pltpu.VMEM((ROWS // 2, COLS), jnp.float32),
                pltpu.VMEM((ROWS // 2, COLS), jnp.float32),
                pltpu.SemaphoreType.DMA((2, 2)),
                pltpu.SemaphoreType.DMA,
            ],
            compiler_params=limit(10),
            cost_estimate=back_cost,
        )(
            place, in_hbm(teacher_exp), in_hbm(student_cap), totals, labels_here,
            in_hbm(student_head), *grads,
        )
        grads.append(grad)
        heads_here.append(head_here)
        theirs.append(swap(out))
    slabs = []
    for part in range(2):
        mine = pl.pallas_call(
            mine_kernel,
            out_shape=[jax.ShapeDtypeStruct((16, 4, D_S // 2), jnp.float32)] * 4,
            in_specs=[smem, vmem, vmem, vmem],
            out_specs=[vmem] * 4,
            scratch_shapes=[pltpu.VMEM((4 * OWN, LANES), jnp.float32)],
            compiler_params=limit(8),
            cost_estimate=back_cost,
        )(place, grads[1], heads_here[part], theirs[part])
        slabs += [mine[0]] + [lax.ppermute(mine[e], AXES, ALONG_LINE[e]) for e in (1, 2, 3)]
    head_grad = pl.pallas_call(
        head_grad_kernel,
        out_shape=pltpu.HBM((D_S, COLS), jnp.bfloat16),
        in_specs=[smem] + [any_space] * 18 + [vmem] * 2,
        out_specs=any_space,
        scratch_shapes=[
            pltpu.VMEM((ROWS, D_ALL), jnp.bfloat16),
            pltpu.VMEM((ROWS, COLS), jnp.bfloat16),
            pltpu.VMEM((2, D_S // HEAD_STEPS, COLS), jnp.bfloat16),
            pltpu.SemaphoreType.DMA((26,)),
            pltpu.SemaphoreType.DMA((2,)),
        ],
        compiler_params=limit(20),
        cost_estimate=pl.CostEstimate(
            flops=2 * ROWS * D_S * COLS, bytes_accessed=13 * MIB, transcendentals=0
        ),
    )(place, *map(in_hbm, pieces), grads[1], grads[0])
    *slabs, head_grad = lax.optimization_barrier((*slabs, head_grad))
    got = pl.pallas_call(
        line_sum_kernel,
        out_shape=pltpu.HBM((16, 4, D_S), jnp.float32),
        in_specs=[vmem] * 8,
        out_specs=any_space,
        scratch_shapes=[
            pltpu.VMEM((16, 4, D_S), jnp.float32),
            pltpu.SemaphoreType.DMA((4,)),
        ],
        compiler_params=limit(6),
    )(*slabs)
    got = lax.all_to_all(got, AXES, 0, 0, tiled=True, axis_index_groups=WALLS)
    hidden = student_hidden.reshape(16, 4, D_S)
    hidden = lax.dynamic_index_in_dim(hidden, 4 * line + other, 0, keepdims=False)
    hidden_grad = pl.pallas_call(
        finish_kernel,
        out_shape=jax.ShapeDtypeStruct((16, 4, D_S), jnp.bfloat16),
        in_specs=[vmem] * 3,
        out_specs=vmem,
        compiler_params=limit(4),
    )(got, hidden, student_gain)
    hidden_grad = lax.all_to_all(hidden_grad, AXES, 0, 0, tiled=True, axis_index_groups=PLANES)

    mine = lax.dynamic_slice_in_dim(totals.reshape(4, ROWS), (4 * core + z) * OWN, OWN, 1)
    divergence = mine[2] / mine[0] - jnp.log(mine[0]) + jnp.log(mine[1])
    loss = KL_WEIGHT * divergence + (1.0 - KL_WEIGHT) * (jnp.log(mine[1]) - mine[3])
    return (loss.reshape(2, 32), hidden_grad.reshape(2, 32, D_S), head_grad)


def solution(mesh):
    in_specs = (
        P(None, "dp", None),
        P(None, "dp", None),
        P(),
        P(),
        P(None, AXES),
        P(None, AXES),
        P(),
    )
    out_specs = (P(None, "dp"), P(None, "dp", None), P(None, AXES))
    return jax.shard_map(body, mesh=mesh, in_specs=in_specs, out_specs=out_specs, check_vma=False)
```

```python
import functools

import jax
import jax.numpy as jnp
from jax import lax
from jax.experimental import pallas as pl
from jax.experimental.pallas import tpu as pltpu
from jax.sharding import PartitionSpec as P

SOFT_CAP = 30.0
KL_WEIGHT = 0.5
NORM_EPS = 1e-06
AXES = ("dp", "sec", "vocab")
D_T, D_S, COLS = 4608, 3584, 1024
D_ALL = D_T + D_S
OWN = 64
ROWS = 8 * OWN
QUARTER = D_ALL // 4
NEAR, FAR = (0, 1, 3), (2,)
FARS = NEAR + FAR
LANES = 896
HEAD_STEPS = 7
MIB = 1024 * 1024


def linear(z, core, x, y):
    return (2 * z + core) * 16 + 4 * x + y


def pairs(move):
    return [
        (linear(z, c, x, y), linear(*move(z, c, x, y)))
        for z in range(4)
        for c in range(2)
        for x in range(4)
        for y in range(4)
    ]


SIBLING = pairs(lambda z, c, x, y: (z, 1 - c, x, y))
ALONG_Z = [pairs(lambda z, c, x, y, d=d: ((z + d) % 4, c, x, y)) for d in range(4)]
ALONG_LINE = [
    pairs(lambda z, c, x, y, e=e: (z, c, x, (y + e) % 4) if c else (z, c, (x + e) % 4, y))
    for e in range(4)
]
CHIPS = [
    [linear(z, c, x, y) for z in range(4) for x in range(4) for y in range(4)] for c in range(2)
]


WALLS = [[linear(z, 0, x, y) for z in range(4) for y in range(4)] for x in range(4)] + [
    [linear(z, 1, x, y) for z in range(4) for x in range(4)] for y in range(4)
]
PLANES = [[linear(z, 0, x, y) for x in range(4) for y in range(4)] for z in range(4)] + [
    [linear(z, 1, x, y) for y in range(4) for x in range(4)] for z in range(4)
]


def swap(value):
    return lax.ppermute(value, AXES, SIBLING)


def norm_kernel(*refs):
    inputs, (own, quarter), buffers, sems = refs[:4], refs[4:6], refs[6:10], refs[10]
    copies = [pltpu.make_async_copy(a, b, sems.at[i]) for i, (a, b) in enumerate(zip(inputs, buffers))]
    begin(copies)
    teacher, student, teacher_gain, student_gain = buffers

    def normed(ref, gain):
        values = ref[...].astype(jnp.float32)
        factor = lax.rsqrt(jnp.mean(values * values, axis=-1, keepdims=True) + NORM_EPS)
        return (values * factor * gain[...][None, :]).astype(jnp.bfloat16)

    finish([copies[1], copies[3]])
    own[:, D_T:] = normed(student, student_gain)
    finish([copies[0], copies[2]])
    own[:, :D_T] = normed(teacher, teacher_gain)
    dp, sec, vocab = (lax.axis_index(a) for a in AXES)
    line = jnp.where(dp % 2 == 0, sec * 2 + vocab // 4, vocab % 4)
    quarter[...] = own[:, pl.ds(pl.multiple_of(line * QUARTER, QUARTER), QUARTER)]


def row_start(place, k, far):
    other = place[1] if k == 0 else 1 - place[1]
    return pl.multiple_of((other * 4 + (place[0] + 4 - far) % 4) * OWN, OWN)


def collect(place, pieces, rows, start_of, sems):
    groups, used = ([], []), 0
    for k, far, sources in pieces:
        block = pl.ds(start_of(k, far), OWN)
        for e, source in enumerate(sources):
            target = rows.at[block]
            if len(sources) > 1:
                lanes = pl.multiple_of(((place[2 + k] + 4 - e) % 4) * QUARTER, QUARTER)
                target = rows.at[block, pl.ds(lanes, QUARTER)]
            groups[k].append(pltpu.make_async_copy(source, target, sems.at[used]))
            used += 1
    return groups


def pieces_of(fars, refs):
    out, per_core = [], len(refs) // 2
    for k in range(2):
        own, lines = refs[k * per_core], refs[(k + 1) * per_core - 4 : (k + 1) * per_core]
        others = [far for far in fars if far]
        for far in fars:
            if far == 0:
                out.append((k, far, [own]))
            else:
                out.append((k, far, [line.at[others.index(far)] for line in lines]))
    return out


def begin(copies):
    for copy in copies:
        copy.start()


def finish(copies):
    for copy in copies:
        copy.wait()


CHUNK = 1536
BUFFERS = 3


def head_chunks(parts, buffers, sems):
    def copy(n):
        head, start, count = parts[n]
        target = buffers.at[n % BUFFERS, pl.ds(0, count), :]
        return pltpu.make_async_copy(head.at[pl.ds(start, count), :], target, sems.at[n % BUFFERS])

    def start(n):
        if n < len(parts):
            copy(n).start()

    return start, lambda n: copy(n).wait()


def all_pieces(refs):
    return pieces_of(NEAR, refs[:10]) + pieces_of(FAR, refs[10:18])


def forward_kernel(place, *refs):
    received, refs = refs[:18], refs[18:]
    teacher_head, student_head, labels = refs[:3]
    teacher_out, student_out, sums = refs[3:6]
    rows, heads, teacher_cap, teacher_exp, student_cap, acc, sems, head_sems, out_sems = refs[6:]
    side = len(FARS) * OWN
    parts = [(teacher_head, at, min(CHUNK, D_T - at)) for at in range(0, D_T, CHUNK)]
    teacher_parts = len(parts)
    parts += [(student_head, at, min(CHUNK, D_S - at)) for at in range(0, D_S, CHUNK)]
    start, wait = head_chunks(parts, heads, head_sems)
    groups = collect(
        place, all_pieces(received), rows, lambda k, far: k * side + FARS.index(far) * OWN, sems
    )
    begin(groups[0])
    start(0)
    begin(groups[1])
    start(1)
    start(2)

    def fold(value):
        return sum(value[:, 128 * i : 128 * i + 128] for i in range(COLS // 128))

    blocks = [(k, far) for k in range(2) for far in FARS]

    def out_copy(source, out, k, b):
        there = pl.ds(row_start(place, *blocks[b]), OWN)
        return pltpu.make_async_copy(source.at[pl.ds(OWN * b, OWN), :], out.at[there, :], out_sems.at[k, b])

    step = 16
    columns = place[4] + lax.broadcasted_iota(jnp.int32, (1, COLS), 1)

    def steps_of(b):
        first = row_start(place, *blocks[b])
        for i in range(OWN // step):
            at = OWN * b + step * i
            yield slice(at, at + step), pl.ds(pl.multiple_of(first + step * i, step), step)

    def teacher_block(b):
        for at, there in steps_of(b):
            t_cap = SOFT_CAP * jnp.tanh(teacher_cap[at, :] * (1.0 / SOFT_CAP))
            t_exp = jnp.exp(t_cap)
            teacher_cap[at, :] = t_cap
            teacher_exp[at, :] = t_exp
            acc[0, there, :] = fold(t_exp)
        out_copy(teacher_exp, teacher_out, 0, b).start()

    def student_block(b):
        for at, there in steps_of(b):
            s_cap = SOFT_CAP * jnp.tanh(student_cap[at, :] * (1.0 / SOFT_CAP))
            student_cap[at, :] = s_cap
            picked = jnp.where(labels[there, :] == columns, s_cap, jnp.float32(0.0))
            acc[1, there, :] = fold(jnp.exp(s_cap))
            acc[2, there, :] = fold(teacher_exp[at, :] * (teacher_cap[at, :] - s_cap))
            acc[3, there, :] = fold(picked)
        out_copy(student_cap, student_out, 1, b).start()

    lane, done = 0, 0
    for n, (_, _, count) in enumerate(parts):
        lanes = slice(lane, lane + count)
        lane += count
        total = teacher_cap if n < teacher_parts else student_cap
        if n == 0:
            for k in range(2):
                finish(groups[k])
                if k == 0:
                    wait(0)
                at = slice(k * side, k * side + side)
                total[at, :] = jnp.dot(
                    rows[at, lanes], heads[0, :count, :], preferred_element_type=jnp.float32
                )
        else:
            wait(n)
            value = jnp.dot(
                rows[:, lanes], heads[n % BUFFERS, :count, :], preferred_element_type=jnp.float32
            )
            total[...] = value if n == teacher_parts else total[...] + value
        if n >= teacher_parts:
            until = len(blocks) * (n + 1 - teacher_parts) // (len(parts) - teacher_parts)
            for b in range(done, until):
                teacher_block(b)
            done = until
        start(n + BUFFERS)
    for b in range(len(blocks)):
        student_block(b)
    for kind in range(4):
        for i in range(4):
            block = acc[kind, 128 * i : 128 * i + 128, :]
            at = 4 * kind + i
            sums[at : at + 1, :] = jnp.sum(block.T, axis=0, keepdims=True)
    for b in range(len(blocks)):
        out_copy(teacher_exp, teacher_out, 0, b).wait()
        out_copy(student_cap, student_out, 1, b).wait()


def back_dot(logit_grad, head, n):
    return lax.dot_general(
        logit_grad[...].reshape(4 * OWN, COLS),
        head[n * LANES : n * LANES + LANES, :],
        (((1,), (1,)), ((), ())),
        preferred_element_type=jnp.float32,
    )


def grad_kernel(part, place, teacher_in, student_in, totals, labels, head, *refs):
    logit_grad, head_here, out, teacher_exp, student_cap, sems, head_sem = refs[part:]
    other = place[1] if part else 1 - place[1]
    first = pl.multiple_of(other * (ROWS // 2), ROWS // 2)
    copies = []
    for i in range(2):
        at, here = pl.ds(pl.multiple_of(first + 128 * i, 128), 128), pl.ds(128 * i, 128)
        copies.append(
            [
                pltpu.make_async_copy(teacher_in.at[at, :], teacher_exp.at[here, :], sems.at[i, 0]),
                pltpu.make_async_copy(student_in.at[at, :], student_cap.at[here, :], sems.at[i, 1]),
            ]
        )
    head_copy = pltpu.make_async_copy(
        head.at[pl.ds(part * (D_S // 2), D_S // 2), :], head_here, head_sem
    )

    def upstream(rows):
        head_copy.wait()
        for n in range(D_S // 2 // LANES):
            out[:, n * LANES : n * LANES + LANES] = back_dot(rows, head_here, n)

    if part:
        head_copy.start()
        for group in copies:
            begin(group)
        upstream(refs[0])
    else:
        for group in copies:
            begin(group)
        head_copy.start()
    columns = place[4] + lax.broadcasted_iota(jnp.int32, (1, COLS), 1)
    for i in range(2):

        def column(kind):
            row = totals[pl.ds(4 * kind + 2 * other + i, 1), :]
            return jnp.broadcast_to(row, (128, 128)).T

        teacher_scale = KL_WEIGHT / column(0)
        student_scale = 1.0 / column(1)
        block = slice(128 * i, 128 * i + 128)
        label = labels[pl.ds(pl.multiple_of(first + 128 * i, 128), 128), :]
        finish(copies[i])
        for j in range(COLS // 128):
            lanes = slice(128 * j, 128 * j + 128)
            s_cap = student_cap[block, lanes]
            ratio = s_cap * (1.0 / SOFT_CAP)
            matches = (label == columns[:, lanes]).astype(jnp.float32)
            grad = (
                jnp.exp(s_cap) * student_scale
                - teacher_exp[block, lanes] * teacher_scale
                - (1.0 - KL_WEIGHT) * matches
            ) * (1.0 - ratio * ratio)
            logit_grad[2 * i, :, lanes] = grad[:OWN].astype(jnp.bfloat16)
            logit_grad[2 * i + 1, :, lanes] = grad[OWN:].astype(jnp.bfloat16)
    if not part:
        upstream(logit_grad)


def head_grad_kernel(place, *refs):
    received = refs[:18]
    mine, theirs, out, rows, logit_grad, buffers, sems, out_sems = refs[18:]
    side = len(FARS) * OWN
    groups = collect(
        place,
        all_pieces(received),
        rows,
        lambda k, far: k * side + pl.multiple_of((place[0] + 4 - far) % 4 * OWN, OWN),
        sems,
    )
    for group in groups:
        begin(group)
    logit_grad[:side, :] = mine[...].reshape(side, COLS)
    logit_grad[side:, :] = theirs[...].reshape(side, COLS)
    for group in groups:
        finish(group)
    step = D_S // HEAD_STEPS

    def copy_out(n):
        return pltpu.make_async_copy(
            buffers.at[n % 2], out.at[pl.ds(step * n, step), :], out_sems.at[n % 2]
        )

    for n in range(HEAD_STEPS):
        lanes = slice(D_T + step * n, D_T + step * n + step)
        value = lax.dot_general(
            rows[:, lanes],
            logit_grad[...],
            (((0,), (0,)), ((), ())),
            preferred_element_type=jnp.float32,
        )
        if n >= 2:
            copy_out(n - 2).wait()
        buffers[n % 2] = value.astype(jnp.bfloat16)
        copy_out(n).start()
    for n in range(HEAD_STEPS - 2, HEAD_STEPS):
        copy_out(n).wait()


def mine_kernel(place, logit_grad, head, received, *rest):
    *outs, value = rest
    for n in range(D_S // 2 // LANES):
        lanes = slice(n * LANES, n * LANES + LANES)
        value[...] = back_dot(logit_grad, head, n) + received[:, lanes]
        for e, out in enumerate(outs):
            for z in range(4):
                at = pl.multiple_of(z * OWN + ((place[2] + e) % 4) * 16, 16)
                block = value[pl.ds(at, 16), :]
                for other in range(4):
                    out[4 * z + other, :, lanes] = block[4 * other : 4 * other + 4]


def line_sum_kernel(*refs):
    slabs, (out, total, sems) = refs[:8], refs[8:]

    def copy_out(i):
        at = pl.ds(4 * i, 4)
        return pltpu.make_async_copy(total.at[at], out.at[at], sems.at[i])

    for i in range(4):
        for part in range(2):
            a, b, c, d = slabs[4 * part : 4 * part + 4]
            lanes = slice(part * (D_S // 2), (part + 1) * (D_S // 2))
            for at in range(4 * i, 4 * i + 4):
                total[at, :, lanes] = (a[at] + b[at]) + (c[at] + d[at])
        copy_out(i).start()
    for i in range(4):
        copy_out(i).wait()


def finish_kernel(got, hidden, gain, out):
    total = got[0]
    for k in range(1, 16):
        total = total + got[k]
    values = hidden[...].astype(jnp.float32)
    factor = lax.rsqrt(jnp.mean(values * values, axis=-1, keepdims=True) + NORM_EPS)
    scaled = total * gain[...][None, :]
    inner_sum = jnp.mean(values * scaled, axis=-1, keepdims=True)
    grad = factor * scaled - values * (factor * factor * factor) * inner_sum
    out[...] = jnp.broadcast_to(grad.astype(jnp.bfloat16)[None], out.shape)


def limit(mib):
    return pltpu.CompilerParams(vmem_limit_bytes=mib * MIB)


def in_hbm(value):
    return pltpu.with_memory_space_constraint(value, pltpu.HBM)


def sum_everywhere(part):
    chip = part + swap(part)
    copies = jnp.broadcast_to(chip[None], (64, 16, 128))
    got = lax.all_to_all(copies, AXES, 0, 0, tiled=True, axis_index_groups=CHIPS)
    return jnp.sum(got, axis=0)


def body(
    teacher_hidden, student_hidden, teacher_gain, student_gain, teacher_head, student_head, labels
):
    dp, sec, vocab = (lax.axis_index(a) for a in AXES)
    z, core = dp // 2, dp % 2
    x, y = sec * 2 + vocab // 4, vocab % 4
    line = jnp.where(core == 0, x, y)
    line_s = other = jnp.where(core == 0, y, x)
    device_place = lax.axis_index(AXES)
    place = jnp.stack([z, core, line, line_s, device_place * COLS, 1 - core]).astype(jnp.int32)
    labels_here = labels.reshape(2, 4, 2, 32).transpose(2, 1, 0, 3).reshape(ROWS, 1)

    smem = pl.BlockSpec(memory_space=pltpu.SMEM)
    vmem = pl.BlockSpec(memory_space=pltpu.VMEM)
    any_space = pl.BlockSpec(memory_space=pltpu.HBM)
    own, quarter = pl.pallas_call(
        norm_kernel,
        out_shape=[
            jax.ShapeDtypeStruct((OWN, D_ALL), jnp.bfloat16),
            jax.ShapeDtypeStruct((OWN, QUARTER), jnp.bfloat16),
        ],
        in_specs=[any_space] * 4,
        out_specs=[vmem] * 2,
        scratch_shapes=[
            pltpu.VMEM((OWN, D_T), jnp.bfloat16),
            pltpu.VMEM((OWN, D_S), jnp.bfloat16),
            pltpu.VMEM((D_T,), jnp.float32),
            pltpu.VMEM((D_S,), jnp.float32),
            pltpu.SemaphoreType.DMA((4,)),
        ],
        compiler_params=limit(10),
    )(
        in_hbm(teacher_hidden.reshape(OWN, D_T)),
        in_hbm(student_hidden.reshape(OWN, D_S)),
        in_hbm(teacher_gain),
        in_hbm(student_gain),
    )

    own_s = swap(own)

    next_1, next_3, opposite = (lax.ppermute(quarter, AXES, ALONG_Z[d]) for d in (1, 3, 2))
    near, own_s = lax.optimization_barrier((jnp.stack([next_1, next_3]), own_s))

    def along_line(value):
        return [value] + [lax.ppermute(value, AXES, ALONG_LINE[e]) for e in (1, 2, 3)]

    near_lines = along_line(near)
    far_lines = along_line(opposite[None])
    pieces = [own, *near_lines, own_s, *map(swap, near_lines), *far_lines, *map(swap, far_lines)]
    teacher_exp, student_cap, sums = pl.pallas_call(
        forward_kernel,
        out_shape=[
            pltpu.HBM((ROWS, COLS), jnp.float32),
            pltpu.HBM((ROWS, COLS), jnp.float32),
            jax.ShapeDtypeStruct((16, 128), jnp.float32),
        ],
        in_specs=[smem] + [any_space] * 20 + [vmem],
        out_specs=[any_space] * 2 + [vmem],
        scratch_shapes=[
            pltpu.VMEM((ROWS, D_ALL), jnp.bfloat16),
            pltpu.VMEM((BUFFERS, CHUNK, COLS), jnp.bfloat16),
            pltpu.VMEM((ROWS, COLS), jnp.float32),
            pltpu.VMEM((ROWS, COLS), jnp.float32),
            pltpu.VMEM((ROWS, COLS), jnp.float32),
            pltpu.VMEM((4, ROWS, 128), jnp.float32),
            pltpu.SemaphoreType.DMA((26,)),
            pltpu.SemaphoreType.DMA((BUFFERS,)),
            pltpu.SemaphoreType.DMA((2, 8)),
        ],
        compiler_params=limit(38),
        cost_estimate=pl.CostEstimate(
            flops=2 * ROWS * D_ALL * COLS, bytes_accessed=30 * MIB, transcendentals=4 * ROWS * COLS
        ),
    )(
        place,
        *map(in_hbm, pieces),
        in_hbm(teacher_head),
        in_hbm(student_head),
        labels_here,
    )

    totals = sum_everywhere(sums)

    back_cost = pl.CostEstimate(
        flops=4 * OWN * COLS * D_S, bytes_accessed=6 * MIB, transcendentals=ROWS * COLS // 2
    )
    grads, heads_here, theirs = [], [], []
    for part in range(2):
        grad, head_here, out = pl.pallas_call(
            functools.partial(grad_kernel, part),
            out_shape=[
                jax.ShapeDtypeStruct((4, OWN, COLS), jnp.bfloat16),
                jax.ShapeDtypeStruct((D_S // 2, COLS), jnp.bfloat16),
                jax.ShapeDtypeStruct((4 * OWN, D_S // 2), jnp.float32),
            ],
            in_specs=[smem] + [any_space] * 2 + [vmem] * 2 + [any_space] + [vmem] * part,
            out_specs=[vmem] * 3,
            scratch_shapes=[
                pltpu.VMEM((ROWS // 2, COLS), jnp.float32),
                pltpu.VMEM((ROWS // 2, COLS), jnp.float32),
                pltpu.SemaphoreType.DMA((2, 2)),
                pltpu.SemaphoreType.DMA,
            ],
            compiler_params=limit(10),
            cost_estimate=back_cost,
        )(
            place, in_hbm(teacher_exp), in_hbm(student_cap), totals, labels_here,
            in_hbm(student_head), *grads,
        )
        grads.append(grad)
        heads_here.append(head_here)
        theirs.append(swap(out))
    slabs = []
    for part in range(2):
        mine = pl.pallas_call(
            mine_kernel,
            out_shape=[jax.ShapeDtypeStruct((16, 4, D_S // 2), jnp.float32)] * 4,
            in_specs=[smem, vmem, vmem, vmem],
            out_specs=[vmem] * 4,
            scratch_shapes=[pltpu.VMEM((4 * OWN, LANES), jnp.float32)],
            compiler_params=limit(8),
            cost_estimate=back_cost,
        )(place, grads[1], heads_here[part], theirs[part])
        slabs += [mine[0]] + [lax.ppermute(mine[e], AXES, ALONG_LINE[e]) for e in (1, 2, 3)]
    head_grad = pl.pallas_call(
        head_grad_kernel,
        out_shape=pltpu.HBM((D_S, COLS), jnp.bfloat16),
        in_specs=[smem] + [any_space] * 18 + [vmem] * 2,
        out_specs=any_space,
        scratch_shapes=[
            pltpu.VMEM((ROWS, D_ALL), jnp.bfloat16),
            pltpu.VMEM((ROWS, COLS), jnp.bfloat16),
            pltpu.VMEM((2, D_S // HEAD_STEPS, COLS), jnp.bfloat16),
            pltpu.SemaphoreType.DMA((26,)),
            pltpu.SemaphoreType.DMA((2,)),
        ],
        compiler_params=limit(20),
        cost_estimate=pl.CostEstimate(
            flops=2 * ROWS * D_S * COLS, bytes_accessed=13 * MIB, transcendentals=0
        ),
    )(place, *map(in_hbm, pieces), grads[1], grads[0])
    *slabs, head_grad = lax.optimization_barrier((*slabs, head_grad))
    got = pl.pallas_call(
        line_sum_kernel,
        out_shape=pltpu.HBM((16, 4, D_S), jnp.float32),
        in_specs=[vmem] * 8,
        out_specs=any_space,
        scratch_shapes=[
            pltpu.VMEM((16, 4, D_S), jnp.float32),
            pltpu.SemaphoreType.DMA((4,)),
        ],
        compiler_params=limit(6),
    )(*slabs)
    got = lax.all_to_all(got, AXES, 0, 0, tiled=True, axis_index_groups=WALLS)
    hidden = student_hidden.reshape(16, 4, D_S)
    hidden = lax.dynamic_index_in_dim(hidden, 4 * line + other, 0, keepdims=False)
    hidden_grad = pl.pallas_call(
        finish_kernel,
        out_shape=jax.ShapeDtypeStruct((16, 4, D_S), jnp.bfloat16),
        in_specs=[vmem] * 3,
        out_specs=vmem,
        compiler_params=limit(4),
    )(got, hidden, student_gain)
    hidden_grad = lax.all_to_all(hidden_grad, AXES, 0, 0, tiled=True, axis_index_groups=PLANES)

    mine = lax.dynamic_slice_in_dim(totals.reshape(4, ROWS), (4 * core + z) * OWN, OWN, 1)
    divergence = mine[2] / mine[0] - jnp.log(mine[0]) + jnp.log(mine[1])
    loss = KL_WEIGHT * divergence + (1.0 - KL_WEIGHT) * (jnp.log(mine[1]) - mine[3])
    return (loss.reshape(2, 32), hidden_grad.reshape(2, 32, D_S), head_grad)


def solution(mesh):
    in_specs = (
        P(None, "dp", None),
        P(None, "dp", None),
        P(),
        P(),
        P(None, AXES),
        P(None, AXES),
        P(),
    )
    out_specs = (P(None, "dp"), P(None, "dp", None), P(None, AXES))
    return jax.shard_map(body, mesh=mesh, in_specs=in_specs, out_specs=out_specs, check_vma=False)
```
